256 devices in a mesh: dp: 8 (over y, z_lo), space: 32 (over x, z_hi, core).
Axes of the slice: x: 4, y: 4, z: 8 (z_hi: 4, z_lo: 2; z = z_hi * 2 + z_lo), core: 2. Of those that a mesh axis runs over, the one named last changes fastest.
Arguments:
- volume: bfloat16 [8, 32, 32, 32, 384], P('dp', 'space'), may hold values from -6 to 6
- gain_one: float32 [384], replicated, may hold values from 0.5 to 1.5
- gain_two: float32 [384], replicated, may hold values from 0.5 to 1.5
- filter_in_weight: float32 [2, 6, 64, 64], replicated, may hold values from -0.75 to 0.75
- filter_in_bias: float32 [2, 6, 64], replicated, may hold values from -3 to 3
- filter_out_weight: float32 [2, 6, 64, 64], replicated, may hold values from -0.75 to 0.75
- filter_out_bias: float32 [2, 6, 64], replicated, may hold values from -3 to 3
- channel_up: bfloat16 [384, 1536], replicated, may hold values from -0.3125 to 0.3125
- channel_up_bias: float32 [1536], replicated, may hold values from -3 to 3
- channel_down: bfloat16 [1536, 384], replicated, may hold values from -0.15625 to 0.15625
- channel_down_bias: float32 [384], replicated, may hold values from -3 to 3
- cotangent: bfloat16 [8, 32, 32, 32, 384], P('dp', 'space'), may hold values from -6 to 6
Outputs:
- result: bfloat16 [8, 32, 32, 32, 384], P('dp', 'space')
- grad_volume: bfloat16 [8, 32, 32, 32, 384], P('dp', 'space')
- grad_gain_one: float32 [384], replicated
- grad_gain_two: float32 [384], replicated
- grad_filter_in_weight: float32 [2, 6, 64, 64], replicated
- grad_filter_in_bias: float32 [2, 6, 64], replicated
- grad_filter_out_weight: float32 [2, 6, 64, 64], replicated
- grad_filter_out_bias: float32 [2, 6, 64], replicated
- grad_channel_up: float32 [384, 1536], P(None, 'space')
- grad_channel_up_bias: float32 [1536], replicated
- grad_channel_down: float32 [1536, 384], P('space')
- grad_channel_down_bias: float32 [384], replicated
The draws below stay inside these ranges and needn't reach their ends.
All inputs are finite; a program needn't handle non-finite values.
Results may differ from the reference program's by a relative error of at most 0.013.
Values sent between devices are 32-bit elements; how exact they have to be, the bound alone decides.
No kernel may reach another device: no remote copies, remote signals or barrier semaphores. Data moves between devices by JAX's collectives and lax.ppermute only.
A program may use at most 128 MiB of HBM per device.

```python
import jax
import jax.numpy as jnp
from jax import lax

WIDTH = 384
BLOCKS = 6
BLOCK = 64
HIDDEN_SIZE = 1536
GY = 32
GZ = 32
KEEP_Y = 16
KEEP_Z = 8
GX = 32
BATCH = 8


def level_of(rng, dims, shards, smallest, top_value):
    def one(dim, parts):
        steps = jax.random.uniform(jax.random.fold_in(jax.random.fold_in(rng, 6), dim), (parts,), jnp.float32, smallest / len(shards), top_value / len(shards))
        return jnp.repeat(jnp.exp(steps), dims[dim] // parts).reshape((-1,) + (1,) * (len(dims) - dim - 1))

    loudness = one(*shards[0])
    for cut in shards[1:]:
        loudness = loudness * one(*cut)
    return loudness


def noise(rng, shape, scale, limit, split=(), kind=jnp.bfloat16):
    values = scale * jax.random.normal(rng, shape, jnp.float32)
    if split:
        values = values * level_of(rng, shape, split, -0.22, 0.18)
    return jnp.clip(values, -limit, limit).astype(kind)


def setup_inputs(seed: int = 0) -> dict:
    arg_keys = jax.random.split(jax.random.key(seed), 13)
    return {
        "volume": noise(arg_keys[0], (BATCH, GX, GY, GZ, WIDTH), 1.0, 6.0, ((0, 8), (1, 32))),
        "gain_one": jnp.clip(1.0 + 0.1 * jax.random.normal(arg_keys[1], (WIDTH,), jnp.float32), 0.5, 1.5),
        "gain_two": jnp.clip(1.0 + 0.1 * jax.random.normal(arg_keys[2], (WIDTH,), jnp.float32), 0.5, 1.5),
        "filter_in_weight": noise(arg_keys[3], (2, BLOCKS, BLOCK, BLOCK), BLOCK ** -0.5, 0.75, (), jnp.float32),
        "filter_in_bias": noise(arg_keys[4], (2, BLOCKS, BLOCK), 0.5, 3.0, (), jnp.float32),
        "filter_out_weight": noise(arg_keys[5], (2, BLOCKS, BLOCK, BLOCK), BLOCK ** -0.5, 0.75, (), jnp.float32),
        "filter_out_bias": noise(arg_keys[6], (2, BLOCKS, BLOCK), 0.5, 3.0, (), jnp.float32),
        "channel_up": noise(arg_keys[7], (WIDTH, HIDDEN_SIZE), WIDTH ** -0.5, 0.3125),
        "channel_up_bias": noise(arg_keys[8], (HIDDEN_SIZE,), 0.5, 3.0, (), jnp.float32),
        "channel_down": noise(arg_keys[9], (HIDDEN_SIZE, WIDTH), HIDDEN_SIZE ** -0.5, 0.15625),
        "channel_down_bias": noise(arg_keys[10], (WIDTH,), 0.5, 3.0, (), jnp.float32),
        "cotangent": noise(arg_keys[11], (BATCH, GX, GY, GZ, WIDTH), 1.0, 6.0, ((0, 8), (1, 32))),
    }


EPSILON = 1e-05
SHRINK = 0.01
PRECISE = lax.Precision.HIGHEST

def layer_norm(values, gain):
    center = values - lax.optimization_barrier(jnp.mean(values, axis=-1, keepdims=True))
    spread = lax.optimization_barrier(jnp.mean(center * center, axis=-1, keepdims=True))
    return center * lax.rsqrt(spread + EPSILON) * gain

def complex_mix(real_part, imag_part, weight, bias):
    real_out = jnp.einsum('...ni,nio->...no', real_part, weight[0], precision=PRECISE) - jnp.einsum('...ni,nio->...no', imag_part, weight[1], precision=PRECISE) + bias[0]
    imag_out = jnp.einsum('...ni,nio->...no', imag_part, weight[0], precision=PRECISE) + jnp.einsum('...ni,nio->...no', real_part, weight[1], precision=PRECISE) + bias[1]
    return (real_out, imag_out)

def soft_shrink(values):
    return values - jnp.clip(values, -SHRINK, SHRINK)

def block_filter(spectrum, in_weight, in_bias, out_weight, out_bias):
    full_shape = spectrum.shape
    split_parts = spectrum.reshape(full_shape[:-1] + (BLOCKS, BLOCK))
    hidden_real, hidden_imag = complex_mix(split_parts[0], split_parts[1], in_weight, in_bias)
    hidden_real = jax.nn.gelu(hidden_real, approximate=True)
    hidden_imag = jax.nn.gelu(hidden_imag, approximate=True)
    out_real, out_imag = complex_mix(hidden_real, hidden_imag, out_weight, out_bias)
    return jnp.stack([soft_shrink(out_real), soft_shrink(out_imag)]).reshape(full_shape)

def kept_rows():
    return jnp.concatenate([jnp.arange(KEEP_Y // 2, dtype=jnp.int32), jnp.arange(GY - KEEP_Y // 2, GY, dtype=jnp.int32)])

def reference(volume, gain_one, gain_two, filter_in_weight, filter_in_bias, filter_out_weight, filter_out_bias, channel_up, channel_up_bias, channel_down, channel_down_bias, cotangent):
    kept_y = kept_rows()
    kept_z = jnp.arange(KEEP_Z, dtype=jnp.int32)
    double_z = jnp.where(kept_z == 0, 1.0, 2.0).astype(gain_one.dtype)
    count_tokens = GX * GY * GZ

    def one_sample(pair):
        sample, upstream_grid = pair
        wide = sample.astype(jnp.float32)
        normed, norm_one_back = jax.vjp(layer_norm, wide, gain_one)
        spectrum_full = jnp.fft.fftn(normed, axes=(0, 1, 2), norm='ortho')
        kept = spectrum_full[:, kept_y][:, :, :KEEP_Z]
        spectrum = jnp.stack([jnp.real(kept), jnp.imag(kept)])
        filtered, filter_back = jax.vjp(block_filter, spectrum, filter_in_weight, filter_in_bias, filter_out_weight, filter_out_bias)
        padded = jnp.zeros((GX, GY, GZ // 2 + 1, WIDTH), spectrum_full.dtype)
        padded = padded.at[:, kept_y[:, None], kept_z[None, :], :].set(lax.complex(filtered[0], filtered[1]))
        filter_out = jnp.fft.irfftn(padded, s=(GX, GY, GZ), axes=(0, 1, 2), norm='ortho')
        mixed = wide + filter_out + normed
        normed_two, norm_two_back = jax.vjp(layer_norm, mixed, gain_two)
        inputs = normed_two.astype(jnp.bfloat16).reshape(count_tokens, WIDTH)
        before = jnp.dot(inputs, channel_up, preferred_element_type=jnp.float32) + channel_up_bias
        hidden = jax.nn.gelu(before, approximate=True).astype(jnp.bfloat16)
        result = (mixed.reshape(count_tokens, WIDTH) + jnp.dot(hidden, channel_down, preferred_element_type=jnp.float32) + channel_down_bias).astype(jnp.bfloat16)
        upstream = upstream_grid.reshape(count_tokens, WIDTH)
        grad_down_bias = lax.optimization_barrier(jnp.sum(upstream.astype(jnp.float32), axis=0))
        grad_down = jnp.dot(hidden.T, upstream, preferred_element_type=jnp.float32)
        grad_hidden = jnp.dot(upstream, channel_down.T, preferred_element_type=jnp.float32)
        gelu_back = jax.vjp(lambda entry: jax.nn.gelu(entry, approximate=True), before)[1]
        grad_before = gelu_back(grad_hidden)[0].astype(jnp.bfloat16)
        grad_up_bias = lax.optimization_barrier(jnp.sum(grad_before.astype(jnp.float32), axis=0))
        grad_up = jnp.dot(inputs.T, grad_before, preferred_element_type=jnp.float32)
        grad_inputs = jnp.dot(grad_before, channel_up.T, preferred_element_type=jnp.float32)
        grad_mixed_norm, grad_gain_two = norm_two_back(grad_inputs.reshape(mixed.shape))
        grad_mixed = upstream.astype(jnp.float32).reshape(mixed.shape) + grad_mixed_norm
        grad_full = jnp.fft.fftn(grad_mixed, axes=(0, 1, 2), norm='ortho')[:, kept_y][:, :, :KEEP_Z]
        grad_spectrum = jnp.stack([jnp.real(grad_full), jnp.imag(grad_full)]) * double_z[:, None]
        grad_in, grad_fw1, grad_fb1, grad_fw2, grad_fb2 = filter_back(grad_spectrum)
        grid = jnp.zeros((GX, GY, GZ, WIDTH), spectrum_full.dtype)
        grid = grid.at[:, kept_y[:, None], kept_z[None, :], :].set(lax.complex(grad_in[0], grad_in[1]))
        grad_normed = jnp.real(jnp.fft.ifftn(grid, axes=(0, 1, 2), norm='ortho')) + grad_mixed
        grad_wide, grad_gain_one = norm_one_back(grad_normed)
        grad_volume = (grad_mixed + grad_wide).astype(jnp.bfloat16)
        return (result.reshape(sample.shape), grad_volume, grad_gain_one, grad_gain_two, grad_fw1, grad_fb1, grad_fw2, grad_fb2, grad_up, grad_up_bias, grad_down, grad_down_bias)
    outputs = lax.map(one_sample, (volume, cotangent))
    summed = [lax.optimization_barrier(jnp.sum(entry, axis=0)) for entry in outputs[2:]]
    return (outputs[0], outputs[1], summed[0], summed[1], summed[2], summed[3], summed[4], summed[5], summed[6], summed[7], summed[8], summed[9])
```

```python
import functools
import math

import jax
import jax.numpy as jnp
import ml_dtypes
import numpy as np
from jax import lax
from jax.experimental import pallas as pl
from jax.experimental.pallas import tpu as pltpu
from jax.sharding import PartitionSpec as P

WIDTH = 384
BLOCKS = 6
BLOCK = 64
HIDDEN = 1536
GX = 32
GY = 32
GZ = 32
KEEP_Y = 16
KEEP_Z = 8
MODES = KEEP_Y * KEEP_Z
OWN = MODES // GX
TOKENS = GY * GZ
PAIRS = BLOCKS // 2
HBLOCK = 256
CHUNK = 256

EPSILON = 1e-05
SHRINK = 0.01
ROOT = math.sqrt(2.0 / math.pi)
CUBIC = 0.044715 * ROOT
VMEM = 60 * 1024 * 1024

BF16 = jnp.bfloat16
F32 = jnp.float32


def halves(table):
    high = table.astype(np.float32).astype(ml_dtypes.bfloat16)
    low = (table - high.astype(np.float64)).astype(np.float32).astype(ml_dtypes.bfloat16)
    return high, low


def slab_table():
    kept = np.concatenate([np.arange(KEEP_Y // 2), np.arange(GY - KEEP_Y // 2, GY)])
    ky, kz = np.repeat(kept, KEEP_Z), np.tile(np.arange(KEEP_Z), KEEP_Y)
    y, z = np.repeat(np.arange(GY), GZ), np.tile(np.arange(GZ), GY)
    steps = (ky[:, None] * y[None, :] * (GZ // math.gcd(GY, GZ)) + kz[:, None] * z[None, :] * (GY // math.gcd(GY, GZ))) % GY
    angle = 2.0 * np.pi * steps / GY
    both = np.stack([np.cos(angle), -np.sin(angle)]).reshape(2, GX, OWN, TOKENS)
    return both.transpose(1, 0, 2, 3).reshape(2 * MODES, TOKENS) / math.sqrt(TOKENS)


def cross_table():
    angle = 2.0 * np.pi * (np.outer(np.arange(GX), np.arange(GX)) % GX) / GX
    cos, sin = np.cos(angle), np.sin(angle)
    table = np.stack([np.stack([cos, sin], -1), np.stack([-sin, cos], -1)])
    full = np.einsum("rkxi,mn->rkmxin", table, np.eye(OWN))
    return full.reshape(2 * GX * OWN, GX * 2 * OWN) / math.sqrt(GX)


def dot(a, b):
    return jnp.dot(a, b, preferred_element_type=F32)


def dot_nt(a, b):
    return lax.dot_general(a, b, (((1,), (1,)), ((), ())), preferred_element_type=F32)


def dot_tn(a, b):
    return lax.dot_general(a, b, (((0,), (0,)), ((), ())), preferred_element_type=F32)


def split(value):
    high = value.astype(BF16)
    return high, (value - high.astype(F32)).astype(BF16)


def dot3(table_high, table_low, value):
    high, low = split(value)
    return dot(table_high, high) + (dot(table_low, high) + dot(table_high, low))


def dot6(a, b):
    return jnp.dot(a, b, preferred_element_type=F32, precision=lax.Precision.HIGHEST)


def normalise(values):
    center = values - jnp.mean(values, axis=-1, keepdims=True)
    rate = lax.rsqrt(jnp.mean(center * center, axis=-1, keepdims=True) + EPSILON)
    return center * rate, rate


def norm_back(grad, unit, rate):
    first = jnp.mean(grad, axis=-1, keepdims=True)
    second = jnp.mean(grad * unit, axis=-1, keepdims=True)
    return rate * (grad - first - unit * second)


def gelu_parts(value):
    square = value * value
    gate = 0.5 + 0.5 * jnp.tanh(value * (ROOT + CUBIC * square))
    active = value * gate
    slope = gate + (active - active * gate) * (2.0 * ROOT + (6.0 * CUBIC) * square)
    return active, slope


def gelu(value):
    return value * (0.5 + 0.5 * jnp.tanh(value * (ROOT + CUBIC * (value * value))))


def mode_weight(shape):
    place = lax.broadcasted_iota(jnp.int32, shape, 0) & (4 * OWN - 1)
    return jnp.where((place == 0) | (place == OWN), 1.0, 2.0).astype(F32)


def first_kernel(volume, table_high, table_low, out):
    unit, _ = normalise(volume[...].astype(F32))
    out[...] = dot3(table_high[...], table_low[...], unit)


def pair_of(value, pair):
    cut = slice(2 * BLOCK * pair, 2 * BLOCK * (pair + 1))
    return jnp.concatenate([value[: GX * OWN, cut], value[GX * OWN :, cut]], axis=1)


def filter_kernel(received, cross_high, cross_low, back_high, back_low, gain, w_in, b_in, w_out, b_out, sent, spectrum, inner, outer):
    unit_spectrum = dot3(cross_high[...], cross_low[...], received[...])
    spectrum[...] = unit_spectrum
    scaled = unit_spectrum * gain[...]
    real, imag = [], []
    for pair in range(PAIRS):
        before = dot6(pair_of(scaled, pair), w_in[pair]) + b_in[pair]
        inner[pair] = before
        after = dot6(gelu(before), w_out[pair]) + b_out[pair]
        outer[pair] = after
        shrunk = after - jnp.clip(after, -SHRINK, SHRINK)
        real.append(shrunk[:, : 2 * BLOCK])
        imag.append(shrunk[:, 2 * BLOCK :])
    filtered = jnp.concatenate([jnp.concatenate(real, axis=1), jnp.concatenate(imag, axis=1)], axis=0)
    sent[...] = dot3(back_high[...], back_low[...], filtered)


def packed_weight(grad):
    half = 2 * BLOCK
    real = grad[:half, :half] + grad[half:, half:]
    imag = grad[:half, half:] - grad[half:, :half]
    lane = lax.broadcasted_iota(jnp.int32, (BLOCK, half), 1)
    return [jnp.where(lane < BLOCK, part[:BLOCK], part[BLOCK:]) for part in (real, imag)]


def filter_back_kernel(received, cross_high, cross_low, back_high, back_low, gain, w_in, w_out, spectrum, inner, outer, sent, grad_w_in, grad_w_out, grad_b_in, grad_b_out, grad_gain):
    grad_spectrum = dot3(cross_high[...], cross_low[...], received[...])
    unit_spectrum = spectrum[...]
    scaled = unit_spectrum * gain[...]
    real, imag = [], []
    for pair in range(PAIRS):
        after = outer[pair]
        grad_out = jnp.where(jnp.abs(after) > SHRINK, pair_of(grad_spectrum, pair), 0.0)
        active, slope = gelu_parts(inner[pair])
        grad_b_out[pair] = jnp.sum(grad_out, axis=0, keepdims=True)
        grad_out = grad_out.astype(BF16)
        grad_w_out[pair, 0], grad_w_out[pair, 1] = packed_weight(dot_tn(active.astype(BF16), grad_out))
        grad_in = dot_nt(grad_out, w_out[pair].astype(BF16)) * slope
        grad_b_in[pair] = jnp.sum(grad_in, axis=0, keepdims=True)
        grad_in = grad_in.astype(BF16)
        grad_w_in[pair, 0], grad_w_in[pair, 1] = packed_weight(dot_tn(pair_of(scaled, pair).astype(BF16), grad_in))
        grad_part = dot_nt(grad_in, w_in[pair].astype(BF16))
        real.append(grad_part[:, : 2 * BLOCK])
        imag.append(grad_part[:, 2 * BLOCK :])
    grad = jnp.concatenate([jnp.concatenate(real, axis=1), jnp.concatenate(imag, axis=1)], axis=0)
    grad_gain[...] = jnp.sum(grad * unit_spectrum, axis=0, keepdims=True)
    sent[...] = dot3(back_high[...], back_low[...], grad)


def mlp_kernel(volume, cotangent, modes, table, table_turned, gain_one, gain_two, up, up_bias, down, down_bias,
               result, grad_mixed, sent, grad_weights, grad_up_bias, sums,
               mixed, unit_one, unit_two, rate_two, inputs, inputs_turned, cotangent_turned, total, grad_inputs):
    step = pl.program_id(0)

    @pl.when(step == 0)
    def _():
        weighted = (modes[...] * mode_weight((2 * MODES, 1))).astype(BF16)
        for at in range(0, TOKENS, CHUNK):
            rows = pl.ds(at, CHUNK)
            wide = volume[rows, :].astype(F32)
            unit, _ = normalise(wide)
            unit_one[rows, :] = unit
            here = wide + dot(table_turned[rows, :], weighted) + unit * gain_one[...]
            mixed[rows, :] = here
            unit, rate = normalise(here)
            unit_two[rows, :] = unit
            rate_two[rows, :] = rate
            rounded = (unit * gain_two[...]).astype(BF16)
            inputs[rows, :] = rounded
            inputs_turned[:, rows] = rounded.T
            cotangent_turned[:, rows] = cotangent[rows, :].T

    hidden_parts, before_parts = [], []
    for at in range(0, TOKENS, CHUNK):
        rows = pl.ds(at, CHUNK)
        before = dot(inputs[rows, :], up[...]) + up_bias[...]
        grad_hidden = dot_nt(cotangent[rows, :], down[...])
        active, slope = gelu_parts(before)
        hidden = active.astype(BF16)
        grad_before = (grad_hidden * slope).astype(BF16)
        hidden_parts.append(hidden)
        before_parts.append(grad_before)
        part = dot(hidden, down[...])
        grad_part = dot_nt(grad_before, up[...])

        @pl.when(step == 0)
        def _():
            total[rows, :] = part
            grad_inputs[rows, :] = grad_part

        @pl.when(step > 0)
        def _():
            total[rows, :] += part
            grad_inputs[rows, :] += grad_part

    hidden = jnp.concatenate(hidden_parts, axis=0)
    grad_before = jnp.concatenate(before_parts, axis=0)
    grad_up_bias[...] = jnp.sum(grad_before.astype(F32), axis=0, keepdims=True)
    grad_weights[:, :WIDTH] = dot(inputs_turned[...], grad_before).T
    grad_weights[:, WIDTH:] = dot(cotangent_turned[...], hidden).T

    @pl.when(step == HIDDEN // HBLOCK - 1)
    def _():
        gain_sum = jnp.zeros((1, WIDTH), F32)
        one_sum = jnp.zeros((1, WIDTH), F32)
        down_sum = jnp.zeros((1, WIDTH), F32)
        spectrum = jnp.zeros((2 * MODES, WIDTH), F32)
        for at in range(0, TOKENS, CHUNK):
            rows = pl.ds(at, CHUNK)
            result[rows, :] = (mixed[rows, :] + total[rows, :] + down_bias[...]).astype(BF16)
            grad = grad_inputs[rows, :]
            unit = unit_two[rows, :]
            gain_sum += jnp.sum(grad * unit, axis=0, keepdims=True)
            upstream = cotangent[rows, :].astype(F32)
            down_sum += jnp.sum(upstream, axis=0, keepdims=True)
            here = upstream + norm_back(grad * gain_two[...], unit, rate_two[rows, :])
            one_sum += jnp.sum(here * unit_one[rows, :], axis=0, keepdims=True)
            grad_mixed[rows, :] = here
            spectrum += dot(table[:, rows], here.astype(BF16))
        sent[...] = spectrum * mode_weight((2 * MODES, 1))
        sums[0:1, :] = gain_sum
        sums[1:2, :] = one_sum
        sums[2:3, :] = down_sum


def last_kernel(volume, modes, table_turned, gain_one, grad_mixed, out):
    rounded = modes[...].astype(BF16)
    for at in range(0, TOKENS, CHUNK):
        rows = pl.ds(at, CHUNK)
        unit, rate = normalise(volume[rows, :].astype(F32))
        here = grad_mixed[rows, :]
        grad = dot(table_turned[rows, :], rounded) + here
        out[rows, :] = (here + norm_back(grad * gain_one[...], unit, rate)).astype(BF16)


def call(kernel, out, *operands):
    return pl.pallas_call(
        kernel,
        out_shape=out,
        compiler_params=pltpu.CompilerParams(vmem_limit_bytes=VMEM),
    )(*operands)


def exchange(value):
    out = lax.all_to_all(value.reshape(GX, 2 * OWN, WIDTH), "space", split_axis=0, concat_axis=0, tiled=True)
    return out.reshape(2 * MODES, WIDTH)


def paired(weight):
    zero = jnp.zeros((PAIRS, BLOCK, BLOCK), F32)
    even, odd = weight[:, 0::2], weight[:, 1::2]

    def wide(index):
        top = jnp.concatenate([even[index], zero], axis=2)
        return jnp.concatenate([top, jnp.concatenate([zero, odd[index]], axis=2)], axis=1)

    real, imag = wide(0), wide(1)
    return jnp.concatenate([jnp.concatenate([real, imag], axis=2), jnp.concatenate([-imag, real], axis=2)], axis=1)


def paired_bias(bias):
    return bias.reshape(2, PAIRS, 2 * BLOCK).transpose(1, 0, 2).reshape(PAIRS, 1, 4 * BLOCK)


def unpaired(grad):
    return grad.reshape(PAIRS, 2, BLOCK, 2, BLOCK).transpose(1, 0, 3, 2, 4).reshape(2, BLOCKS, BLOCK, BLOCK)


def unpaired_bias(grad):
    return grad.reshape(PAIRS, 2, 2, BLOCK).transpose(1, 0, 2, 3).reshape(2, BLOCKS, BLOCK)


def local(volume, gain_one, gain_two, w_in, b_in, w_out, b_out, up, up_bias, down, down_bias, cotangent):
    shape = volume.shape
    volume = volume.reshape(TOKENS, WIDTH)
    cotangent = cotangent.reshape(TOKENS, WIDTH)
    gain_one, gain_two, down_bias = (value.reshape(1, WIDTH) for value in (gain_one, gain_two, down_bias))
    slab = slab_table()
    slab_high, slab_low = (jnp.asarray(part) for part in halves(slab))
    slab_turned = jnp.asarray(halves(slab.T)[0])
    cross = cross_table()
    cross_high, cross_low = (jnp.asarray(part) for part in halves(cross))
    back_high, back_low = (jnp.asarray(part) for part in halves(cross.T))
    w_in, w_out, b_in, b_out = paired(w_in), paired(w_out), paired_bias(b_in), paired_bias(b_out)

    def sds(*dims, dtype=F32):
        return jax.ShapeDtypeStruct(dims, dtype)

    modes = call(first_kernel, sds(2 * MODES, WIDTH), volume, slab_high, slab_low)
    modes = exchange(modes)
    wide = sds(PAIRS, GX * OWN, 4 * BLOCK)
    modes, spectrum, inner, outer = call(
        filter_kernel,
        (sds(2 * MODES, WIDTH), sds(2 * MODES, WIDTH), wide, wide),
        modes, cross_high, cross_low, back_high, back_low, gain_one, w_in, b_in, w_out, b_out,
    )
    modes = exchange(modes)

    def whole(*dims):
        return pl.BlockSpec(dims, lambda step: (0,) * len(dims))

    steps = HIDDEN // HBLOCK
    result, grad_mixed, modes, grad_weights, grad_up_bias, sums = pl.pallas_call(
        mlp_kernel,
        grid=(steps,),
        in_specs=[
            whole(TOKENS, WIDTH), whole(TOKENS, WIDTH), whole(2 * MODES, WIDTH), whole(2 * MODES, TOKENS), whole(TOKENS, 2 * MODES),
            whole(1, WIDTH), whole(1, WIDTH),
            pl.BlockSpec((WIDTH, HBLOCK), lambda step: (0, step)),
            pl.BlockSpec((1, HBLOCK), lambda step: (0, step)),
            pl.BlockSpec((HBLOCK, WIDTH), lambda step: (step, 0)),
            whole(1, WIDTH),
        ],
        out_specs=(
            whole(TOKENS, WIDTH), whole(TOKENS, WIDTH), whole(2 * MODES, WIDTH),
            pl.BlockSpec((HBLOCK, 2 * WIDTH), lambda step: (step, 0)),
            pl.BlockSpec((1, HBLOCK), lambda step: (0, step)),
            whole(8, WIDTH),
        ),
        out_shape=(
            sds(TOKENS, WIDTH, dtype=BF16), sds(TOKENS, WIDTH), sds(2 * MODES, WIDTH),
            sds(HIDDEN, 2 * WIDTH), sds(1, HIDDEN), sds(8, WIDTH),
        ),
        scratch_shapes=[
            pltpu.VMEM((TOKENS, WIDTH), F32), pltpu.VMEM((TOKENS, WIDTH), F32), pltpu.VMEM((TOKENS, WIDTH), F32),
            pltpu.VMEM((TOKENS, 1), F32), pltpu.VMEM((TOKENS, WIDTH), BF16),
            pltpu.VMEM((WIDTH, TOKENS), BF16), pltpu.VMEM((WIDTH, TOKENS), BF16),
            pltpu.VMEM((TOKENS, WIDTH), F32), pltpu.VMEM((TOKENS, WIDTH), F32),
        ],
        compiler_params=pltpu.CompilerParams(vmem_limit_bytes=VMEM),
    )(volume, cotangent, modes, slab_high, slab_turned, gain_one, gain_two, up, up_bias.reshape(1, HIDDEN), down, down_bias)

    grad_weights = lax.psum_scatter(grad_weights, "space", scatter_dimension=0, tiled=True)
    modes = exchange(modes)
    packed = sds(PAIRS, 2, BLOCK, 2 * BLOCK)
    row = sds(PAIRS, 1, 4 * BLOCK)
    modes, grad_w_in, grad_w_out, grad_b_in, grad_b_out, grad_gain = call(
        filter_back_kernel,
        (sds(2 * MODES, WIDTH), packed, packed, row, row, sds(1, WIDTH)),
        modes, cross_high, cross_low, back_high, back_low, gain_one, w_in, w_out, spectrum, inner, outer,
    )
    modes = exchange(modes)
    grad_volume = call(last_kernel, sds(TOKENS, WIDTH, dtype=BF16), volume, modes, slab_turned, gain_one, grad_mixed)
    grad_weights = lax.psum(grad_weights, "dp")
    summed = lax.psum(
        (grad_w_in, grad_w_out, grad_b_in, grad_b_out, grad_gain[0] + sums[1], sums[0], sums[2], grad_up_bias[0]), ("dp", "space")
    )
    return (
        result.reshape(shape),
        grad_volume.reshape(shape),
        summed[4],
        summed[5],
        unpaired(summed[0]),
        unpaired_bias(summed[2]),
        unpaired(summed[1]),
        unpaired_bias(summed[3]),
        grad_weights[:, :WIDTH].T,
        summed[7],
        grad_weights[:, WIDTH:],
        summed[6],
    )


def solution(mesh):
    field = P("dp", "space", None, None, None)
    return jax.shard_map(
        local,
        mesh=mesh,
        in_specs=(field,) + (P(),) * 10 + (field,),
        out_specs=(field, field) + (P(),) * 6 + (P(None, "space"), P(), P("space", None), P()),
        check_vma=False,
    )
```

```python
import functools
import math

import jax
import jax.numpy as jnp
import ml_dtypes
import numpy as np
from jax import lax
from jax.experimental import pallas as pl
from jax.experimental.pallas import tpu as pltpu
from jax.sharding import PartitionSpec as P

WIDTH = 384
BLOCKS = 6
BLOCK = 64
HIDDEN = 1536
GX = 32
GY = 32
GZ = 32
KEEP_Y = 16
KEEP_Z = 8
MODES = KEEP_Y * KEEP_Z
OWN = MODES // GX
TOKENS = GY * GZ
PAIRS = BLOCKS // 2
HBLOCK = 256
CHUNK = 256

Y_CORE = [
    [(y * 2 + low) * GX + place * 2 + core for y in range(4) for core in range(2)] for low in range(2) for place in range(GX // 2)
]
X_Z = [[place * 2 + core for place in range(GX // 2)] for core in range(2)]

EPSILON = 1e-05
SHRINK = 0.01
ROOT = math.sqrt(2.0 / math.pi)
CUBIC = 0.044715 * ROOT
MIB = 1024 * 1024

BF16 = jnp.bfloat16
F32 = jnp.float32


def halves(table):
    high = table.astype(np.float32).astype(ml_dtypes.bfloat16)
    low = (table - high.astype(np.float64)).astype(np.float32).astype(ml_dtypes.bfloat16)
    return high, low


def slab_table():
    kept = np.concatenate([np.arange(KEEP_Y // 2), np.arange(GY - KEEP_Y // 2, GY)])
    ky, kz = np.repeat(kept, KEEP_Z), np.tile(np.arange(KEEP_Z), KEEP_Y)
    y, z = np.repeat(np.arange(GY), GZ), np.tile(np.arange(GZ), GY)
    steps = (ky[:, None] * y[None, :] * (GZ // math.gcd(GY, GZ)) + kz[:, None] * z[None, :] * (GY // math.gcd(GY, GZ))) % GY
    angle = 2.0 * np.pi * steps / GY
    both = np.stack([np.cos(angle), -np.sin(angle)]).reshape(2, GX, OWN, TOKENS)
    return both.transpose(1, 0, 2, 3).reshape(2 * MODES, TOKENS) / math.sqrt(TOKENS)


def cross_table():
    angle = 2.0 * np.pi * (np.outer(np.arange(GX), np.arange(GX)) % GX) / GX
    cos, sin = np.cos(angle), np.sin(angle)
    table = np.stack([np.stack([cos, sin], -1), np.stack([-sin, cos], -1)])
    full = np.einsum("rkxi,mn->rkmxin", table, np.eye(OWN))
    return full.reshape(2 * GX * OWN, GX * 2 * OWN) / math.sqrt(GX)


def dot(a, b):
    return jnp.dot(a, b, preferred_element_type=F32)


def dot_nt(a, b):
    return lax.dot_general(a, b, (((1,), (1,)), ((), ())), preferred_element_type=F32)


def dot_tn(a, b):
    return lax.dot_general(a, b, (((0,), (0,)), ((), ())), preferred_element_type=F32)


def split(value):
    high = value.astype(BF16)
    return high, (value - high.astype(F32)).astype(BF16)


def dot3(table_high, table_low, value):
    high, low = split(value)
    return dot(table_high, high) + (dot(table_low, high) + dot(table_high, low))


def dot6(a, b):
    return jnp.dot(a, b, preferred_element_type=F32, precision=lax.Precision.HIGHEST)


def normalise(values):
    center = values - jnp.mean(values, axis=-1, keepdims=True)
    rate = lax.rsqrt(jnp.mean(center * center, axis=-1, keepdims=True) + EPSILON)
    return center * rate, rate


def norm_back(grad, unit, rate):
    first = jnp.mean(grad, axis=-1, keepdims=True)
    second = jnp.mean(grad * unit, axis=-1, keepdims=True)
    return rate * (grad - first - unit * second)


def gelu_parts(value):
    square = value * value
    gate = 0.5 + 0.5 * jnp.tanh(value * (ROOT + CUBIC * square))
    active = value * gate
    slope = gate + (active - active * gate) * (2.0 * ROOT + (6.0 * CUBIC) * square)
    return active, slope


def gelu(value):
    return value * (0.5 + 0.5 * jnp.tanh(value * (ROOT + CUBIC * (value * value))))


def mode_weight(shape):
    place = lax.broadcasted_iota(jnp.int32, shape, 0) & (4 * OWN - 1)
    return jnp.where((place == 0) | (place == OWN), 1.0, 2.0).astype(F32)


def first_kernel(volume, table_high, table_low, out):
    unit, _ = normalise(volume[...].astype(F32))
    out[...] = dot3(table_high[...], table_low[...], unit)


def pair_of(value, pair):
    cut = slice(2 * BLOCK * pair, 2 * BLOCK * (pair + 1))
    return jnp.concatenate([value[: GX * OWN, cut], value[GX * OWN :, cut]], axis=1)


def filter_kernel(received, cross_high, cross_low, back_high, back_low, gain, w_in, b_in, w_out, b_out, sent, spectrum, inner, outer):
    unit_spectrum = dot3(cross_high[...], cross_low[...], received[...])
    spectrum[...] = unit_spectrum
    scaled = unit_spectrum * gain[...]
    real, imag = [], []
    for pair in range(PAIRS):
        before = dot6(pair_of(scaled, pair), w_in[pair]) + b_in[pair]
        inner[pair] = before
        after = dot6(gelu(before), w_out[pair]) + b_out[pair]
        outer[pair] = after
        shrunk = after - jnp.clip(after, -SHRINK, SHRINK)
        real.append(shrunk[:, : 2 * BLOCK])
        imag.append(shrunk[:, 2 * BLOCK :])
    filtered = jnp.concatenate([jnp.concatenate(real, axis=1), jnp.concatenate(imag, axis=1)], axis=0)
    sent[...] = dot3(back_high[...], back_low[...], filtered)


def packed_weight(grad):
    half = 2 * BLOCK
    real = grad[:half, :half] + grad[half:, half:]
    imag = grad[:half, half:] - grad[half:, :half]
    lane = lax.broadcasted_iota(jnp.int32, (BLOCK, half), 1)
    return [jnp.where(lane < BLOCK, part[:BLOCK], part[BLOCK:]) for part in (real, imag)]


SMALL = 40


def filter_back_kernel(received, cross_high, cross_low, back_high, back_low, gain, w_in, w_out, spectrum, inner, outer, sums, up_sum, sent, small):
    half = 2 * BLOCK
    grad_spectrum = dot3(cross_high[...], cross_low[...], received[...])
    unit_spectrum = spectrum[...]
    scaled = unit_spectrum * gain[...]
    real, imag, weights = [], [], [[], []]
    small[...] = jnp.zeros((GX * 8, half), F32)
    for pair in range(PAIRS):
        after = outer[pair]
        grad_out = jnp.where(jnp.abs(after) > SHRINK, pair_of(grad_spectrum, pair), 0.0)
        active, slope = gelu_parts(inner[pair])
        bias = jnp.sum(grad_out, axis=0, keepdims=True)
        small[6 + 2 * pair : 7 + 2 * pair, :] = bias[:, :half]
        small[7 + 2 * pair : 8 + 2 * pair, :] = bias[:, half:]
        grad_out = grad_out.astype(BF16)
        weights[1] += packed_weight(dot_tn(active.astype(BF16), grad_out))
        grad_in = dot_nt(grad_out, w_out[pair].astype(BF16)) * slope
        bias = jnp.sum(grad_in, axis=0, keepdims=True)
        small[2 * pair : 1 + 2 * pair, :] = bias[:, :half]
        small[1 + 2 * pair : 2 + 2 * pair, :] = bias[:, half:]
        grad_in = grad_in.astype(BF16)
        weights[0] += packed_weight(dot_tn(pair_of(scaled, pair).astype(BF16), grad_in))
        grad_part = dot_nt(grad_in, w_in[pair].astype(BF16))
        real.append(grad_part[:, :half])
        imag.append(grad_part[:, half:])
    grad = jnp.concatenate([jnp.concatenate(real, axis=1), jnp.concatenate(imag, axis=1)], axis=0)
    gain_grad = jnp.sum(grad * unit_spectrum, axis=0, keepdims=True) + sums[1:2, :]
    for at in range(3):
        lanes = slice(at * half, (at + 1) * half)
        small[12 + at : 13 + at, :] = gain_grad[:, lanes]
        small[15 + at : 16 + at, :] = sums[0:1, lanes]
        small[18 + at : 19 + at, :] = sums[2:3, lanes]
    for at in range(HIDDEN // half):
        small[21 + at : 22 + at, :] = up_sum[0:1, at * half : (at + 1) * half]
    sent[:, :, :WIDTH] = dot3(back_high[...], back_low[...], grad).reshape(GX, 8, WIDTH)
    for which in range(2):
        for at, part in enumerate(weights[which]):
            for group in range(8):
                place = (which * 2 * PAIRS + at) * 8 + group
                lanes = WIDTH + (place % 3) * half
                sent[place // 3, :, lanes : lanes + half] = part[group * 8 : group * 8 + 8, :]
    sent[:, :, WIDTH + 3 * half :] = small[...].reshape(GX, 8, half)


def mlp_kernel(volume, cotangent, modes, table, table_turned, gain_one, gain_two, up, up_bias, down,
               mixed, inputs, hidden, grad_before, grad_mixed, sent, up_sum, sums, weighted):
    step = pl.program_id(0)

    @pl.when(step == 0)
    def _():
        weighted[...] = (modes[...] * mode_weight((2 * MODES, 1))).astype(BF16)
        sent[...] = jnp.zeros_like(sent)
        up_sum[...] = jnp.zeros_like(up_sum)
        sums[...] = jnp.zeros_like(sums)

    wide = volume[...].astype(F32)
    unit_one, _ = normalise(wide)
    mixed_here = wide + dot(table_turned[...], weighted[...]) + unit_one * gain_one[...]
    mixed[...] = mixed_here
    unit_two, rate_two = normalise(mixed_here)
    inputs_here = (unit_two * gain_two[...]).astype(BF16)
    inputs[...] = inputs_here
    upstream = cotangent[...]
    grad = jnp.zeros((CHUNK, WIDTH), F32)
    for at in range(0, HIDDEN, HBLOCK):
        cut = slice(at, at + HBLOCK)
        before = dot(inputs_here, up[:, cut]) + up_bias[:, cut]
        active, slope = gelu_parts(before)
        hidden[:, cut] = active.astype(BF16)
        back = (dot_nt(upstream, down[cut, :]) * slope).astype(BF16)
        grad_before[:, cut] = back
        up_sum[0:1, cut] += jnp.sum(back.astype(F32), axis=0, keepdims=True)
    grad = dot_nt(grad_before[...], up[...])
    upstream = upstream.astype(F32)
    grad_here = upstream + norm_back(grad * gain_two[...], unit_two, rate_two)
    grad_mixed[...] = grad_here
    sums[0:1, :] += jnp.sum(grad * unit_two, axis=0, keepdims=True)
    sums[1:2, :] += jnp.sum(grad_here * unit_one, axis=0, keepdims=True)
    sums[2:3, :] += jnp.sum(upstream, axis=0, keepdims=True)
    sent[...] += dot(table[...], grad_here.astype(BF16)) * mode_weight((2 * MODES, 1))


WBLOCK = 768


def weight_kernel(mixed, inputs, cotangent, hidden, grad_before, down, down_bias, result, terms, total):
    step = pl.program_id(0)
    part = dot(hidden[...], down[...])

    @pl.when(step == 0)
    def _():
        total[...] = mixed[...] + down_bias[...] + part

    @pl.when(step == HIDDEN // WBLOCK - 1)
    def _():
        result[...] = (total[...] + part).astype(BF16)

    for which, (left, right) in enumerate(((grad_before, inputs), (hidden, cotangent))):
        term = dot_tn(left[...], right[...])
        for place in range(WBLOCK // 96):
            for core in range(2):
                for half in range(2):
                    at = place * 96 + core * 48 + half * 24
                    terms[which * 2 + half, core, place] = term[at : at + 24, :]


def last_kernel(volume, received, table_turned, gain_one, grad_mixed, out, rounded):
    @pl.when(pl.program_id(0) == 0)
    def _():
        rounded[...] = received[:, :, :WIDTH].reshape(2 * MODES, WIDTH).astype(BF16)

    unit, rate = normalise(volume[...].astype(F32))
    here = grad_mixed[...]
    grad = dot(table_turned[...], rounded[...]) + here
    out[...] = (here + norm_back(grad * gain_one[...], unit, rate)).astype(BF16)


def first_sum_kernel(received, out):
    total = jnp.sum(received[:, :, WIDTH:], axis=0)
    for copy in range(8):
        out[copy] = total


def second_sum_kernel(received, terms, out):
    total = jnp.sum(received[...], axis=0)
    for place in range(GX // 2):
        for group in range(3):
            out[place, :, group * WIDTH : (group + 1) * WIDTH] = terms[place, group * 8 : group * 8 + 8, :]
        out[place, :, 3 * WIDTH :] = total


def third_sum_kernel(received, out, slices):
    for group in range(3):
        total = jnp.sum(received[:, :, group * WIDTH : (group + 1) * WIDTH], axis=0)
        for copy in range(8):
            out[copy, group * 8 : group * 8 + 8, :] = total
    slices[...] = received[:, :, 3 * WIDTH :]


def final_kernel(core, received, mine, other, grad_up, grad_down, grad_w_in, grad_w_out, grad_b_in, grad_b_out, grad_one, grad_two, grad_down_bias, grad_up_bias, small):
    half = 2 * BLOCK
    parts = [received[2 * y] + received[2 * y + 1] for y in range(4)]
    grad_up[...] = jnp.concatenate(parts[:2], axis=0)
    grad_down[...] = jnp.concatenate(parts[2:], axis=0)
    first = core[0] == 0
    even = jnp.where(first, mine[...], other[...])
    odd = jnp.where(first, other[...], mine[...])
    both = (even, odd)
    for which, out in enumerate((grad_w_in, grad_w_out)):
        for at in range(2 * PAIRS):
            for group in range(8):
                place = (which * 2 * PAIRS + at) * 8 + group
                owner, lanes = place // 3, (place % 3) * half
                tile = both[owner % 2][owner // 2, :, lanes : lanes + half]
                rows = slice(group * 8, group * 8 + 8)
                out[at % 2, 2 * (at // 2), rows, :] = tile[:, :BLOCK]
                out[at % 2, 2 * (at // 2) + 1, rows, :] = tile[:, BLOCK:]
    for owner in range(SMALL // 8):
        small[owner * 8 : owner * 8 + 8, :] = both[owner % 2][owner // 2, :, 3 * half :]
    for first, out in ((0, grad_b_in), (6, grad_b_out)):
        for pair in range(PAIRS):
            for part in range(2):
                row = small[first + 2 * pair + part : first + 2 * pair + part + 1, :]
                out[2 * pair, part : part + 1, :] = row[:, :BLOCK]
                out[2 * pair + 1, part : part + 1, :] = row[:, BLOCK:]
    for first, out in ((12, grad_one), (15, grad_two), (18, grad_down_bias), (21, grad_up_bias)):
        for at in range(out.shape[0] // half):
            out[at * half : (at + 1) * half] = small[first + at, :]


def limit(mib):
    return pltpu.CompilerParams(vmem_limit_bytes=mib * MIB)


def call(kernel, out, *operands):
    return pl.pallas_call(kernel, out_shape=out, compiler_params=limit(12))(*operands)


def exchange(value, axis, groups=None):
    return lax.all_to_all(value, axis, split_axis=0, concat_axis=0, axis_index_groups=groups, tiled=True)


def paired(weight):
    zero = jnp.zeros((PAIRS, BLOCK, BLOCK), F32)
    even, odd = weight[:, 0::2], weight[:, 1::2]

    def wide(index):
        top = jnp.concatenate([even[index], zero], axis=2)
        return jnp.concatenate([top, jnp.concatenate([zero, odd[index]], axis=2)], axis=1)

    real, imag = wide(0), wide(1)
    return jnp.concatenate([jnp.concatenate([real, imag], axis=2), jnp.concatenate([-imag, real], axis=2)], axis=1)


def paired_bias(bias):
    return bias.reshape(2, PAIRS, 2 * BLOCK).transpose(1, 0, 2).reshape(PAIRS, 1, 4 * BLOCK)


def local(volume, gain_one, gain_two, w_in, b_in, w_out, b_out, up, up_bias, down, down_bias, cotangent):
    shape = volume.shape
    volume = volume.reshape(TOKENS, WIDTH)
    cotangent = cotangent.reshape(TOKENS, WIDTH)
    gain_one, gain_two, down_bias = (value.reshape(1, WIDTH) for value in (gain_one, gain_two, down_bias))
    slab = slab_table()
    slab_high, slab_low = (jnp.asarray(part) for part in halves(slab))
    slab_turned = jnp.asarray(halves(slab.T)[0])
    cross = cross_table()
    cross_high, cross_low = (jnp.asarray(part) for part in halves(cross))
    back_high, back_low = (jnp.asarray(part) for part in halves(cross.T))
    w_in, w_out, b_in, b_out = paired(w_in), paired(w_out), paired_bias(b_in), paired_bias(b_out)

    def sds(*dims, dtype=F32):
        return jax.ShapeDtypeStruct(dims, dtype)

    def slab(value):
        return value.reshape(GX, 2 * OWN, WIDTH)

    def rows(value):
        return value.reshape(2 * MODES, WIDTH)

    modes = call(first_kernel, sds(2 * MODES, WIDTH), volume, slab_high, slab_low)
    modes = rows(exchange(slab(modes), "space"))
    wide = sds(PAIRS, GX * OWN, 4 * BLOCK)
    modes, spectrum, inner, outer = call(
        filter_kernel,
        (sds(2 * MODES, WIDTH), sds(2 * MODES, WIDTH), wide, wide),
        modes, cross_high, cross_low, back_high, back_low, gain_one, w_in, b_in, w_out, b_out,
    )
    modes = rows(exchange(slab(modes), "space"))

    def whole(*dims):
        return pl.BlockSpec(dims, lambda step: (0,) * len(dims))

    def chunk(*dims):
        return pl.BlockSpec(dims, lambda step: (step, 0))

    def across(*dims):
        return pl.BlockSpec(dims, lambda step: (0, step))

    mixed, inputs, hidden, grad_before, grad_mixed, modes, up_sum, sums = pl.pallas_call(
        mlp_kernel,
        grid=(TOKENS // CHUNK,),
        in_specs=[
            chunk(CHUNK, WIDTH), chunk(CHUNK, WIDTH), whole(2 * MODES, WIDTH), across(2 * MODES, CHUNK), chunk(CHUNK, 2 * MODES),
            whole(1, WIDTH), whole(1, WIDTH), whole(WIDTH, HIDDEN), whole(1, HIDDEN), whole(HIDDEN, WIDTH),
        ],
        out_specs=(
            chunk(CHUNK, WIDTH), chunk(CHUNK, WIDTH), chunk(CHUNK, HIDDEN), chunk(CHUNK, HIDDEN), chunk(CHUNK, WIDTH),
            whole(2 * MODES, WIDTH), whole(8, HIDDEN), whole(8, WIDTH),
        ),
        out_shape=(
            sds(TOKENS, WIDTH), sds(TOKENS, WIDTH, dtype=BF16), sds(TOKENS, HIDDEN, dtype=BF16), sds(TOKENS, HIDDEN, dtype=BF16),
            sds(TOKENS, WIDTH), sds(2 * MODES, WIDTH), sds(8, HIDDEN), sds(8, WIDTH),
        ),
        scratch_shapes=[pltpu.VMEM((2 * MODES, WIDTH), BF16)],
        compiler_params=limit(60),
    )(volume, cotangent, modes, slab_high, slab_turned, gain_one, gain_two, up, up_bias.reshape(1, HIDDEN), down)

    places = GX // 2
    result, terms = pl.pallas_call(
        weight_kernel,
        grid=(HIDDEN // WBLOCK,),
        in_specs=[
            whole(TOKENS, WIDTH), whole(TOKENS, WIDTH), whole(TOKENS, WIDTH), across(TOKENS, WBLOCK), across(TOKENS, WBLOCK),
            chunk(WBLOCK, WIDTH), whole(1, WIDTH),
        ],
        out_specs=(
            whole(TOKENS, WIDTH),
            pl.BlockSpec((4, 2, WBLOCK // 96, 24, WIDTH), lambda step: (0, 0, step, 0, 0)),
        ),
        out_shape=(sds(TOKENS, WIDTH, dtype=BF16), sds(4, 2, places, 24, WIDTH)),
        scratch_shapes=[pltpu.VMEM((TOKENS, WIDTH), F32)],
        compiler_params=limit(60),
        cost_estimate=pl.CostEstimate(flops=6 * TOKENS * WIDTH * HIDDEN, bytes_accessed=16 * 1024 * 1024, transcendentals=0),
    )(mixed, inputs, cotangent, hidden, grad_before, down, down_bias)

    modes = exchange(slab(modes), "space")
    terms, modes = lax.optimization_barrier((terms, modes))
    terms = lax.psum_scatter(
        terms.reshape(8, places * 24, WIDTH), ("dp", "space"), scatter_dimension=0, axis_index_groups=Y_CORE, tiled=True
    ).reshape(places, 24, WIDTH)
    modes = rows(modes)
    carried = 3 * 2 * BLOCK + 2 * BLOCK
    sent = pl.pallas_call(
        filter_back_kernel,
        out_shape=sds(GX, 8, WIDTH + carried),
        scratch_shapes=[pltpu.VMEM((GX * 8, 2 * BLOCK), F32)],
        compiler_params=limit(12),
    )(modes, cross_high, cross_low, back_high, back_low, gain_one, w_in, w_out, spectrum, inner, outer, sums, up_sum)
    received = exchange(sent, "space")
    shared = exchange(call(first_sum_kernel, sds(8, 8, carried), received), "dp")
    grad_volume = pl.pallas_call(
        last_kernel,
        grid=(TOKENS // CHUNK,),
        in_specs=[
            chunk(CHUNK, WIDTH), pl.BlockSpec((GX, 8, WIDTH + carried), lambda step: (0, 0, 0)), chunk(CHUNK, 2 * MODES), whole(1, WIDTH), chunk(CHUNK, WIDTH),
        ],
        out_specs=chunk(CHUNK, WIDTH),
        out_shape=sds(TOKENS, WIDTH, dtype=BF16),
        scratch_shapes=[pltpu.VMEM((2 * MODES, WIDTH), BF16)],
        compiler_params=limit(12),
        cost_estimate=pl.CostEstimate(flops=TOKENS * WIDTH * 1024, bytes_accessed=8 * 1024 * 1024, transcendentals=0),
    )(volume, received, slab_turned, gain_one, grad_mixed)
    gathered = exchange(call(second_sum_kernel, sds(places, 8, 3 * WIDTH + carried), shared, terms), "space", X_Z)
    copies, mine = call(third_sum_kernel, (sds(8, 24, WIDTH), sds(places, 8, carried)), gathered)
    other = lax.ppermute(mine, "space", [(at, at ^ 1) for at in range(GX)])
    copies = exchange(copies, "dp")
    core = (lax.axis_index("space") & 1).reshape(1)
    square = sds(2, BLOCKS, BLOCK, BLOCK)
    vmem = pl.BlockSpec(memory_space=pltpu.VMEM)
    tall = sds(BLOCKS, 2, BLOCK)
    row = sds(WIDTH)
    grad_up, grad_down, grad_w_in, grad_w_out, grad_b_in, grad_b_out, grad_one, grad_two, grad_down_bias, grad_up_bias = pl.pallas_call(
        final_kernel,
        in_specs=[pl.BlockSpec(memory_space=pltpu.SMEM), vmem, vmem, vmem],
        out_shape=(sds(48, WIDTH), sds(48, WIDTH), square, square, tall, tall, row, row, row, sds(HIDDEN)),
        scratch_shapes=[pltpu.VMEM((SMALL, 2 * BLOCK), F32)],
        compiler_params=limit(8),
    )(core, copies, mine, other)
    return (
        result.reshape(shape),
        grad_volume.reshape(shape),
        grad_one,
        grad_two,
        grad_w_in,
        grad_b_in.transpose(1, 0, 2),
        grad_w_out,
        grad_b_out.transpose(1, 0, 2),
        grad_up.T,
        grad_up_bias,
        grad_down,
        grad_down_bias,
    )


def solution(mesh):
    field = P("dp", "space", None, None, None)
    return jax.shard_map(
        local,
        mesh=mesh,
        in_specs=(field,) + (P(),) * 10 + (field,),
        out_specs=(field, field) + (P(),) * 6 + (P(None, "space"), P(), P("space", None), P()),
        check_vma=False,
    )
```

```python
import functools
import math

import jax
import jax.numpy as jnp
import ml_dtypes
import numpy as np
from jax import lax
from jax.experimental import pallas as pl
from jax.experimental.pallas import tpu as pltpu
from jax.sharding import PartitionSpec as P

WIDTH = 384
BLOCKS = 6
BLOCK = 64
HIDDEN = 1536
GX = 32
GY = 32
GZ = 32
KEEP_Y = 16
KEEP_Z = 8
MODES = KEEP_Y * KEEP_Z
PLACES = GX // 2
OWN = MODES // PLACES
TOKENS = GY * GZ
HALF = BLOCKS // 2
PAIR = 2 * BLOCK
HBLOCK = 256
CHUNK = 512

Y_CORE = [
    [(y * 2 + low) * GX + place * 2 + core for y in range(4) for core in range(2)] for low in range(2) for place in range(GX // 2)
]
X_Z = [[place * 2 + core for place in range(GX // 2)] for core in range(2)]

EPSILON = 1e-05
SHRINK = 0.01
ROOT = math.sqrt(2.0 / math.pi)
CUBIC = 0.044715 * ROOT
MIB = 1024 * 1024
LATE = 200_000_000_000

BF16 = jnp.bfloat16
F32 = jnp.float32


def halves(table):
    high = table.astype(np.float32).astype(ml_dtypes.bfloat16)
    low = (table - high.astype(np.float64)).astype(np.float32).astype(ml_dtypes.bfloat16)
    return high, low


def slab_table():
    kept = np.concatenate([np.arange(KEEP_Y // 2), np.arange(GY - KEEP_Y // 2, GY)])
    ky, kz = np.repeat(kept, KEEP_Z), np.tile(np.arange(KEEP_Z), KEEP_Y)
    y, z = np.repeat(np.arange(GY), GZ), np.tile(np.arange(GZ), GY)
    angle = 2.0 * np.pi * ((ky[:, None] * y[None, :] + kz[:, None] * z[None, :]) % GY) / GY
    both = np.stack([np.cos(angle), -np.sin(angle)]).reshape(2, PLACES, OWN, TOKENS)
    return both.transpose(1, 0, 2, 3).reshape(2 * MODES, TOKENS) / math.sqrt(TOKENS)


def cross_tables():
    angle = 2.0 * np.pi * (np.outer(np.arange(GX), np.arange(GX)) % GX) / GX
    return [np.kron(part(angle), np.eye(OWN)) / math.sqrt(GX) for part in (np.cos, np.sin)]


def dot(a, b):
    return jnp.dot(a, b, preferred_element_type=F32)


def dot_nt(a, b):
    return lax.dot_general(a, b, (((1,), (1,)), ((), ())), preferred_element_type=F32)


def dot_tn(a, b):
    return lax.dot_general(a, b, (((0,), (0,)), ((), ())), preferred_element_type=F32)


def split(value):
    high = value.astype(BF16)
    return high, (value - high.astype(F32)).astype(BF16)


def dot3(table_high, table_low, value):
    high, low = split(value)
    return dot(table_high, high) + (dot(table_low, high) + dot(table_high, low))


def dot6(a, b):
    return jnp.dot(a, b, preferred_element_type=F32, precision=lax.Precision.HIGHEST)


def normalise(values):
    center = values - jnp.mean(values, axis=-1, keepdims=True)
    rate = lax.rsqrt(jnp.mean(center * center, axis=-1, keepdims=True) + EPSILON)
    return center * rate, rate


def norm_back(grad, unit, rate):
    first = jnp.mean(grad, axis=-1, keepdims=True)
    second = jnp.mean(grad * unit, axis=-1, keepdims=True)
    return rate * (grad - first - unit * second)


def gelu_parts(value):
    square = value * value
    gate = 0.5 + 0.5 * jnp.tanh(value * (ROOT + CUBIC * square))
    active = value * gate
    slope = gate + (active - active * gate) * (2.0 * ROOT + (6.0 * CUBIC) * square)
    return active, slope


def gelu(value):
    return value * (0.5 + 0.5 * jnp.tanh(value * (ROOT + CUBIC * (value * value))))


def mode_weight():
    place = lax.broadcasted_iota(jnp.int32, (2 * MODES, 1), 0) & (KEEP_Z - 1)
    return jnp.where(place == 0, 1.0, 2.0).astype(F32)


def low_lanes(rows):
    return lax.broadcasted_iota(jnp.int32, (rows, PAIR), 1) < BLOCK


def turn(tile):
    return pltpu.roll(tile, BLOCK, 1)


def tiles(value):
    return [value[:, at : at + PAIR] for at in range(0, value.shape[1], PAIR)]


def to_owners(value, out):
    value = value.reshape(PLACES, 2, OWN, WIDTH)
    low = low_lanes(MODES)
    for at, (real, imag) in enumerate(zip(tiles(value[:, 0].reshape(MODES, WIDTH)), tiles(value[:, 1].reshape(MODES, WIDTH)))):
        for block, tile in ((2 * at, jnp.where(low, real, turn(imag))), (2 * at + 1, jnp.where(low, turn(real), imag))):
            lanes = (block % HALF) * PAIR
            out[:, block // HALF, :, lanes : lanes + PAIR] = tile.reshape(PLACES, OWN, PAIR)


def from_owners(value):
    low = low_lanes(MODES)
    blocks = [tile for core in range(2) for tile in tiles(value[:, core].reshape(MODES, WIDTH))]
    real = [jnp.where(low, even, turn(odd)) for even, odd in zip(blocks[0::2], blocks[1::2])]
    imag = [jnp.where(low, turn(even), odd) for even, odd in zip(blocks[0::2], blocks[1::2])]
    parts = [jnp.concatenate(part, axis=1).reshape(PLACES, 1, OWN, WIDTH) for part in (real, imag)]
    return jnp.concatenate(parts, axis=1).reshape(2 * MODES, WIDTH)


def times_minus_i(value):
    low = low_lanes(value.shape[0])
    return jnp.concatenate([jnp.where(low, turn(tile), -turn(tile)) for tile in tiles(value)], axis=1)


def along_x(tables, value, sign):
    cos_high, cos_low, sin_high, sin_low = (table[...] for table in tables)
    straight = dot3(cos_high, cos_low, value)
    crossed = dot3(sin_high, sin_low, times_minus_i(value))
    return straight + crossed if sign < 0 else straight - crossed


def first_kernel(volume, table_high, table_low, out):
    unit, _ = normalise(volume[...].astype(F32))
    to_owners(dot3(table_high[...], table_low[...], unit), out)


def filter_kernel(received, cos_high, cos_low, sin_high, sin_low, gain, w_in, b_in, w_out, b_out, sent, spectrum, inner, outer):
    tables = (cos_high, cos_low, sin_high, sin_low)
    unit_spectrum = along_x(tables, received[...], -1)
    spectrum[...] = unit_spectrum
    shrunk = []
    for block, part in enumerate(tiles(unit_spectrum * gain[...])):
        before = dot6(part, w_in[block]) + b_in[block]
        inner[block] = before
        after = dot6(gelu(before), w_out[block]) + b_out[block]
        outer[block] = after
        shrunk.append(after - jnp.clip(after, -SHRINK, SHRINK))
    sent[...] = along_x(tables, jnp.concatenate(shrunk, axis=1), 1)


def packed_weight(grad):
    other = turn(grad[BLOCK:])
    return grad[:BLOCK] + jnp.where(low_lanes(BLOCK), other, -other)


SMALL = 32


def filter_back_kernel(received, cos_high, cos_low, sin_high, sin_low, gain, w_in, w_out, spectrum, inner, outer, sums, up_sum, sent, weights, small):
    tables = (cos_high, cos_low, sin_high, sin_low)
    unit_spectrum = spectrum[...]
    small[...] = jnp.zeros_like(small)
    grads = []
    scaled = tiles(unit_spectrum * gain[...])
    for block, grad_out in enumerate(tiles(along_x(tables, received[...], -1))):
        grad_out = jnp.where(jnp.abs(outer[block]) > SHRINK, grad_out, 0.0)
        active, slope = gelu_parts(inner[block])
        small[HALF + block : HALF + block + 1, :] = jnp.sum(grad_out, axis=0, keepdims=True)
        grad_out = grad_out.astype(BF16)
        weights[HALF + block] = packed_weight(dot_tn(active.astype(BF16), grad_out))
        grad_in = dot_nt(grad_out, w_out[block].astype(BF16)) * slope
        small[block : block + 1, :] = jnp.sum(grad_in, axis=0, keepdims=True)
        grad_in = grad_in.astype(BF16)
        weights[block] = packed_weight(dot_tn(scaled[block].astype(BF16), grad_in))
        grads.append(dot_nt(grad_in, w_in[block].astype(BF16)))
    grad = jnp.concatenate(grads, axis=1)
    for block, part in enumerate(tiles(jnp.sum(grad * unit_spectrum, axis=0, keepdims=True))):
        row = jnp.broadcast_to(part, (8, PAIR))
        small[6 + block : 7 + block, :] = (row + turn(row))[0:1, :]
    for at in range(3):
        lanes = slice(at * PAIR, (at + 1) * PAIR)
        small[9 + at : 10 + at, :] = sums[1:2, lanes]
        small[12 + at : 13 + at, :] = sums[0:1, lanes]
        small[15 + at : 16 + at, :] = sums[2:3, lanes]
    for at in range(HIDDEN // PAIR):
        small[18 + at : 19 + at, :] = up_sum[0:1, at * PAIR : (at + 1) * PAIR]
    sent[:, :, :WIDTH] = along_x(tables, grad, 1).reshape(GX, 8, WIDTH)
    for owner in range(GX):
        at = owner * 8
        sent[owner, :, WIDTH : WIDTH + PAIR] = weights[at // BLOCK, at % BLOCK : at % BLOCK + 8, :]
        at = GX * 8 + owner * 4
        sent[owner, 0:4, WIDTH + PAIR :] = weights[at // BLOCK, at % BLOCK : at % BLOCK + 4, :]
        if owner * 4 < SMALL:
            sent[owner, 4:8, WIDTH + PAIR :] = small[owner * 4 : owner * 4 + 4, :]
        else:
            sent[owner, 4:8, WIDTH + PAIR :] = jnp.zeros((4, PAIR), F32)


def mlp_kernel(volume, cotangent, modes, table, table_turned, gain_one, gain_two, up, up_bias, down,
               mixed, inputs, hidden, grad_before, grad_mixed, sent, up_sum, sums):
    weighted = (from_owners(modes[...]) * mode_weight()).astype(BF16)
    wide = volume[...].astype(F32)
    unit_one, _ = normalise(wide)
    mixed_here = wide + dot(table_turned[...], weighted) + unit_one * gain_one[...]
    mixed[...] = mixed_here
    unit_two, rate_two = normalise(mixed_here)
    inputs_here = (unit_two * gain_two[...]).astype(BF16)
    inputs[...] = inputs_here
    upstream = cotangent[...]
    up_sum[...] = jnp.zeros_like(up_sum)
    for at in range(0, HIDDEN, HBLOCK):
        cut = slice(at, at + HBLOCK)
        before = dot(inputs_here, up[:, cut]) + up_bias[:, cut]
        active, slope = gelu_parts(before)
        hidden[:, cut] = active.astype(BF16)
        back = (dot_nt(upstream, down[cut, :]) * slope).astype(BF16)
        grad_before[:, cut] = back
        up_sum[0:1, cut] = jnp.sum(back.astype(F32), axis=0, keepdims=True)
    grad = dot_nt(grad_before[...], up[...])
    upstream = upstream.astype(F32)
    grad_here = upstream + norm_back(grad * gain_two[...], unit_two, rate_two)
    grad_mixed[...] = grad_here
    sums[...] = jnp.zeros_like(sums)
    sums[0:1, :] = jnp.sum(grad * unit_two, axis=0, keepdims=True)
    sums[1:2, :] = jnp.sum(grad_here * unit_one, axis=0, keepdims=True)
    sums[2:3, :] = jnp.sum(upstream, axis=0, keepdims=True)
    to_owners(dot(table[...], grad_here.astype(BF16)) * mode_weight(), sent)


WBLOCK = 768


def weight_kernel(inputs, cotangent, hidden, grad_before, terms):
    for which, (left, right) in enumerate(((grad_before, inputs), (hidden, cotangent))):
        term = dot_tn(left[...], right[...])
        for place in range(WBLOCK // 96):
            for core in range(2):
                for half in range(2):
                    at = place * 96 + core * 48 + half * 24
                    terms[which * 2 + half, core, place] = term[at : at + 24, :]


def result_kernel(mixed, hidden, down, down_bias, result):
    result[...] = (mixed[...] + down_bias[...] + dot(hidden[...], down[...])).astype(BF16)


def last_kernel(volume, received, table_turned, gain_one, grad_mixed, out, rounded):
    @pl.when(pl.program_id(0) == 0)
    def _():
        rounded[...] = from_owners(received[:, :, :, :WIDTH]).astype(BF16)

    unit, rate = normalise(volume[...].astype(F32))
    here = grad_mixed[...]
    grad = dot(table_turned[...], rounded[...]) + here
    out[...] = (here + norm_back(grad * gain_one[...], unit, rate)).astype(BF16)


def first_sum_kernel(received, out):
    total = jnp.concatenate([jnp.sum(received[:, core, :, WIDTH:], axis=0) for core in range(2)], axis=1)
    for copy in range(8):
        out[copy] = total


def second_sum_kernel(received, terms, out):
    total = jnp.sum(received[...], axis=0)
    for place in range(PLACES):
        for group in range(3):
            out[place, :, group * WIDTH : (group + 1) * WIDTH] = terms[place, group * 8 : group * 8 + 8, :]
        out[place, :, 3 * WIDTH :] = total


def third_sum_kernel(received, out, slices):
    for group in range(3):
        total = jnp.sum(received[:, :, group * WIDTH : (group + 1) * WIDTH], axis=0)
        for copy in range(8):
            out[copy, group * 8 : group * 8 + 8, :] = total
    slices[...] = received[:, :, 3 * WIDTH :]


def final_kernel(core, received, mine, other, grad_up, grad_down, grad_w_in, grad_w_out, grad_b_in, grad_b_out, grad_one, grad_two, grad_down_bias, grad_up_bias, weights, small):
    parts = [received[2 * y] + received[2 * y + 1] for y in range(4)]
    grad_up[...] = jnp.concatenate(parts[:2], axis=0)
    grad_down[...] = jnp.concatenate(parts[2:], axis=0)
    first = core[0] == 0
    both = (jnp.where(first, mine[...], other[...]), jnp.where(first, other[...], mine[...]))
    for owner in range(GX):
        piece = both[owner % 2][owner // 2]
        for half in range(2):
            lanes = 2 * PAIR * half
            weights[half, owner * 8 : owner * 8 + 8, :] = piece[:, lanes : lanes + PAIR]
            at = GX * 8 + owner * 4
            weights[half, at : at + 4, :] = piece[0:4, lanes + PAIR : lanes + 2 * PAIR]
            if owner * 4 < SMALL:
                small[half, owner * 4 : owner * 4 + 4, :] = piece[4:8, lanes + PAIR : lanes + 2 * PAIR]
    for which, out in enumerate((grad_w_in, grad_w_out)):
        for block in range(BLOCKS):
            at = (which * HALF + block % HALF) * BLOCK
            part = weights[block // HALF, at : at + BLOCK, :]
            out[0, block] = part[:, :BLOCK]
            out[1, block] = part[:, BLOCK:]
    for first_row, out in ((0, grad_b_in), (HALF, grad_b_out)):
        for block in range(BLOCKS):
            row = small[block // HALF, first_row + block % HALF : first_row + block % HALF + 1, :]
            out[block, 0:1, :] = row[:, :BLOCK]
            out[block, 1:2, :] = row[:, BLOCK:]
    tokens = small[0] + small[1]
    low = low_lanes(1)
    for at in range(3):
        even, odd = (small[block // HALF, 6 + block % HALF : 7 + block % HALF, :] for block in (2 * at, 2 * at + 1))
        row = tokens[9 + at : 10 + at, :] + jnp.where(low, even, odd)
        grad_one[at * PAIR : (at + 1) * PAIR] = row[0]
    for first_row, out in ((12, grad_two), (15, grad_down_bias), (18, grad_up_bias)):
        for at in range(out.shape[0] // PAIR):
            out[at * PAIR : (at + 1) * PAIR] = tokens[first_row + at]


def limit(mib):
    return pltpu.CompilerParams(vmem_limit_bytes=mib * MIB)


def call(kernel, out, *operands, mib=12):
    return pl.pallas_call(kernel, out_shape=out, compiler_params=limit(mib))(*operands)


def exchange(value, axis, groups=None):
    return lax.all_to_all(value, axis, split_axis=0, concat_axis=0, axis_index_groups=groups, tiled=True)


def paired(weight, core):
    weight = lax.dynamic_slice_in_dim(weight, core * HALF, HALF, 1)
    top = jnp.concatenate([weight[0], weight[1]], axis=2)
    return jnp.concatenate([top, jnp.concatenate([-weight[1], weight[0]], axis=2)], axis=1)


def paired_bias(bias, core):
    bias = lax.dynamic_slice_in_dim(bias, core * HALF, HALF, 1)
    return bias.transpose(1, 0, 2).reshape(HALF, 1, PAIR)


def local(volume, gain_one, gain_two, w_in, b_in, w_out, b_out, up, up_bias, down, down_bias, cotangent):
    shape = volume.shape
    volume = volume.reshape(TOKENS, WIDTH)
    cotangent = cotangent.reshape(TOKENS, WIDTH)
    gain_one, gain_two, down_bias = (value.reshape(1, WIDTH) for value in (gain_one, gain_two, down_bias))
    slab = slab_table()
    slab_high, slab_low = (jnp.asarray(part) for part in halves(slab))
    slab_turned = jnp.asarray(halves(slab.T)[0])
    cross = [jnp.asarray(part) for table in cross_tables() for part in halves(table)]
    core = lax.axis_index("space") & 1
    w_in, w_out, b_in, b_out = paired(w_in, core), paired(w_out, core), paired_bias(b_in, core), paired_bias(b_out, core)
    gain = lax.dynamic_slice_in_dim(gain_one.reshape(BLOCKS, 1, BLOCK), core * HALF, HALF, 0)
    gain = jnp.broadcast_to(gain, (HALF, 2, BLOCK)).reshape(1, WIDTH)

    def sds(*dims, dtype=F32):
        return jax.ShapeDtypeStruct(dims, dtype)

    def rows(value):
        return value.reshape(2 * MODES, WIDTH)

    def places(value):
        return value.reshape(PLACES, 2, OWN, value.shape[-1])

    def owners(value):
        return value.reshape(GX, OWN, WIDTH)

    wave = sds(PLACES, 2, OWN, WIDTH)
    modes = call(first_kernel, wave, volume, slab_high, slab_low, mib=60)
    modes = rows(exchange(owners(modes), "space"))
    wide = sds(HALF, 2 * MODES, PAIR)
    modes, spectrum, inner, outer = call(
        filter_kernel, (sds(2 * MODES, WIDTH), sds(2 * MODES, WIDTH), wide, wide), modes, *cross, gain, w_in, b_in, w_out, b_out
    )
    modes = places(exchange(owners(modes), "space"))

    def whole(*dims):
        return pl.BlockSpec(dims, lambda step: (0,) * len(dims))

    def chunk(*dims):
        return pl.BlockSpec(dims, lambda step: (step, 0))

    def across(*dims):
        return pl.BlockSpec(dims, lambda step: (0, step))

    mixed, inputs, hidden, grad_before, grad_mixed, modes, up_sum, sums = call(
        mlp_kernel,
        (
            sds(TOKENS, WIDTH), sds(TOKENS, WIDTH, dtype=BF16), sds(TOKENS, HIDDEN, dtype=BF16), sds(TOKENS, HIDDEN, dtype=BF16),
            sds(TOKENS, WIDTH), wave, sds(8, HIDDEN), sds(8, WIDTH),
        ),
        volume, cotangent, modes, slab_high, slab_turned, gain_one, gain_two, up, up_bias.reshape(1, HIDDEN), down,
        mib=60,
    )

    terms = pl.pallas_call(
        weight_kernel,
        grid=(HIDDEN // WBLOCK,),
        in_specs=[whole(TOKENS, WIDTH), whole(TOKENS, WIDTH), across(TOKENS, WBLOCK), across(TOKENS, WBLOCK)],
        out_specs=pl.BlockSpec((4, 2, WBLOCK // 96, 24, WIDTH), lambda step: (0, 0, step, 0, 0)),
        out_shape=sds(4, 2, PLACES, 24, WIDTH),
        compiler_params=limit(60),
        cost_estimate=pl.CostEstimate(flops=4 * TOKENS * WIDTH * HIDDEN, bytes_accessed=12 * MIB, transcendentals=0),
    )(inputs, cotangent, hidden, grad_before)
    result = pl.pallas_call(
        result_kernel,
        grid=(TOKENS // CHUNK,),
        in_specs=[chunk(CHUNK, WIDTH), chunk(CHUNK, HIDDEN), whole(HIDDEN, WIDTH), whole(1, WIDTH)],
        out_specs=chunk(CHUNK, WIDTH),
        out_shape=sds(TOKENS, WIDTH, dtype=BF16),
        compiler_params=limit(60),
        cost_estimate=pl.CostEstimate(flops=2 * TOKENS * WIDTH * HIDDEN, bytes_accessed=7 * MIB, transcendentals=0),
    )(mixed, hidden, down, down_bias)

    modes = exchange(owners(modes), "space")
    terms = lax.psum_scatter(
        terms.reshape(8, PLACES * 24, WIDTH), ("dp", "space"), scatter_dimension=0, axis_index_groups=Y_CORE, tiled=True
    ).reshape(PLACES, 24, WIDTH)
    modes = rows(modes)
    carried = 2 * PAIR
    sent = pl.pallas_call(
        filter_back_kernel,
        out_shape=sds(GX, 8, WIDTH + carried),
        scratch_shapes=[pltpu.VMEM((2 * HALF, BLOCK, PAIR), F32), pltpu.VMEM((SMALL, PAIR), F32)],
        compiler_params=limit(12),
        cost_estimate=pl.CostEstimate(flops=LATE, bytes_accessed=8 * MIB, transcendentals=0),
    )(modes, *cross, gain, w_in, w_out, spectrum, inner, outer, sums, up_sum)
    received = places(exchange(sent, "space"))
    shared = exchange(call(first_sum_kernel, sds(8, 8, 2 * carried), received), "dp")
    grad_volume = pl.pallas_call(
        last_kernel,
        grid=(TOKENS // CHUNK,),
        in_specs=[
            chunk(CHUNK, WIDTH), whole(PLACES, 2, OWN, WIDTH + carried), chunk(CHUNK, 2 * MODES), whole(1, WIDTH), chunk(CHUNK, WIDTH),
        ],
        out_specs=chunk(CHUNK, WIDTH),
        out_shape=sds(TOKENS, WIDTH, dtype=BF16),
        scratch_shapes=[pltpu.VMEM((2 * MODES, WIDTH), BF16)],
        compiler_params=limit(12),
        cost_estimate=pl.CostEstimate(flops=TOKENS * WIDTH * 1024, bytes_accessed=8 * 1024 * 1024, transcendentals=0),
    )(volume, received, slab_turned, gain_one, grad_mixed)
    gathered = exchange(call(second_sum_kernel, sds(PLACES, 8, 3 * WIDTH + 2 * carried), shared, terms), "space", X_Z)
    copies, mine = call(third_sum_kernel, (sds(8, 24, WIDTH), sds(PLACES, 8, 2 * carried)), gathered)
    other = lax.ppermute(mine, "space", [(at, at ^ 1) for at in range(GX)])
    copies = exchange(copies, "dp")
    square = sds(2, BLOCKS, BLOCK, BLOCK)
    vmem = pl.BlockSpec(memory_space=pltpu.VMEM)
    tall = sds(BLOCKS, 2, BLOCK)
    row = sds(WIDTH)
    grad_up, grad_down, grad_w_in, grad_w_out, grad_b_in, grad_b_out, grad_one, grad_two, grad_down_bias, grad_up_bias = pl.pallas_call(
        final_kernel,
        in_specs=[pl.BlockSpec(memory_space=pltpu.SMEM), vmem, vmem, vmem],
        out_shape=(sds(48, WIDTH), sds(48, WIDTH), square, square, tall, tall, row, row, row, sds(HIDDEN)),
        scratch_shapes=[pltpu.VMEM((2, 2 * HALF * BLOCK, PAIR), F32), pltpu.VMEM((2, SMALL, PAIR), F32)],
        compiler_params=limit(8),
    )(core.reshape(1), copies, mine, other)
    return (
        result.reshape(shape),
        grad_volume.reshape(shape),
        grad_one,
        grad_two,
        grad_w_in,
        grad_b_in.transpose(1, 0, 2),
        grad_w_out,
        grad_b_out.transpose(1, 0, 2),
        grad_up.T,
        grad_up_bias,
        grad_down,
        grad_down_bias,
    )


def solution(mesh):
    field = P("dp", "space", None, None, None)
    return jax.shard_map(
        local,
        mesh=mesh,
        in_specs=(field,) + (P(),) * 10 + (field,),
        out_specs=(field, field) + (P(),) * 6 + (P(None, "space"), P(), P("space", None), P()),
        check_vma=False,
    )
```

```python
import functools
import math

import jax
import jax.numpy as jnp
import ml_dtypes
import numpy as np
from jax import lax
from jax.experimental import pallas as pl
from jax.experimental.pallas import tpu as pltpu
from jax.sharding import PartitionSpec as P

WIDTH = 384
BLOCKS = 6
BLOCK = 64
HIDDEN = 1536
GX = 32
GY = 32
GZ = 32
KEEP_Y = 16
KEEP_Z = 8
MODES = KEEP_Y * KEEP_Z
PLACES = GX // 2
OWN = MODES // PLACES
TOKENS = GY * GZ
HALF = BLOCKS // 2
PAIR = 2 * BLOCK
HBLOCK = 256
CHUNK = 512

Y_CORE = [
    [(y * 2 + low) * GX + place * 2 + core for y in range(4) for core in range(2)] for low in range(2) for place in range(GX // 2)
]
X_Z = [[place * 2 + core for place in range(GX // 2)] for core in range(2)]

EPSILON = 1e-05
SHRINK = 0.01
ROOT = math.sqrt(2.0 / math.pi)
CUBIC = 0.044715 * ROOT
MIB = 1024 * 1024
LATE = 200_000_000_000

BF16 = jnp.bfloat16
F32 = jnp.float32


def halves(table):
    high = table.astype(np.float32).astype(ml_dtypes.bfloat16)
    low = (table - high.astype(np.float64)).astype(np.float32).astype(ml_dtypes.bfloat16)
    return high, low


def slab_table():
    kept = np.concatenate([np.arange(KEEP_Y // 2), np.arange(GY - KEEP_Y // 2, GY)])
    ky, kz = np.repeat(kept, KEEP_Z), np.tile(np.arange(KEEP_Z), KEEP_Y)
    y, z = np.repeat(np.arange(GY), GZ), np.tile(np.arange(GZ), GY)
    angle = 2.0 * np.pi * ((ky[:, None] * y[None, :] + kz[:, None] * z[None, :]) % GY) / GY
    both = np.stack([np.cos(angle), -np.sin(angle)]).reshape(2, PLACES, OWN, TOKENS)
    return both.transpose(1, 0, 2, 3).reshape(2 * MODES, TOKENS) / math.sqrt(TOKENS)


def cross_tables():
    angle = 2.0 * np.pi * (np.outer(np.arange(GX), np.arange(GX)) % GX) / GX
    return [np.kron(part(angle), np.eye(OWN)) / math.sqrt(GX) for part in (np.cos, np.sin)]


def dot(a, b):
    return jnp.dot(a, b, preferred_element_type=F32)


def dot_nt(a, b):
    return lax.dot_general(a, b, (((1,), (1,)), ((), ())), preferred_element_type=F32)


def dot_tn(a, b):
    return lax.dot_general(a, b, (((0,), (0,)), ((), ())), preferred_element_type=F32)


def split(value):
    high = value.astype(BF16)
    return high, (value - high.astype(F32)).astype(BF16)


def dot3(table_high, table_low, value):
    high, low = split(value)
    return dot(table_high, high) + (dot(table_low, high) + dot(table_high, low))


def dot6(a, b):
    return jnp.dot(a, b, preferred_element_type=F32, precision=lax.Precision.HIGHEST)


def normalise(values):
    center = values - jnp.mean(values, axis=-1, keepdims=True)
    rate = lax.rsqrt(jnp.mean(center * center, axis=-1, keepdims=True) + EPSILON)
    return center * rate, rate


def norm_back(grad, unit, rate):
    first = jnp.mean(grad, axis=-1, keepdims=True)
    second = jnp.mean(grad * unit, axis=-1, keepdims=True)
    return rate * (grad - first - unit * second)


def gelu_parts(value):
    square = value * value
    gate = 0.5 + 0.5 * jnp.tanh(value * (ROOT + CUBIC * square))
    active = value * gate
    slope = gate + (active - active * gate) * (2.0 * ROOT + (6.0 * CUBIC) * square)
    return active, slope


def gelu(value):
    return value * (0.5 + 0.5 * jnp.tanh(value * (ROOT + CUBIC * (value * value))))


def mode_weight():
    place = lax.broadcasted_iota(jnp.int32, (2 * MODES, 1), 0) & (KEEP_Z - 1)
    return jnp.where(place == 0, 1.0, 2.0).astype(F32)


def low_lanes(rows):
    return lax.broadcasted_iota(jnp.int32, (rows, PAIR), 1) < BLOCK


def turn(tile):
    return pltpu.roll(tile, BLOCK, 1)


def tiles(value):
    return [value[:, at : at + PAIR] for at in range(0, value.shape[1], PAIR)]


def to_owners(value, out):
    value = value.reshape(PLACES, 2, OWN, WIDTH)
    low = low_lanes(MODES)
    for at, (real, imag) in enumerate(zip(tiles(value[:, 0].reshape(MODES, WIDTH)), tiles(value[:, 1].reshape(MODES, WIDTH)))):
        for block, tile in ((2 * at, jnp.where(low, real, turn(imag))), (2 * at + 1, jnp.where(low, turn(real), imag))):
            lanes = (block % HALF) * PAIR
            out[:, block // HALF, :, lanes : lanes + PAIR] = tile.reshape(PLACES, OWN, PAIR)


def from_owners(value):
    low = low_lanes(MODES)
    blocks = [tile for core in range(2) for tile in tiles(value[:, core].reshape(MODES, WIDTH))]
    real = [jnp.where(low, even, turn(odd)) for even, odd in zip(blocks[0::2], blocks[1::2])]
    imag = [jnp.where(low, turn(even), odd) for even, odd in zip(blocks[0::2], blocks[1::2])]
    parts = [jnp.concatenate(part, axis=1).reshape(PLACES, 1, OWN, WIDTH) for part in (real, imag)]
    return jnp.concatenate(parts, axis=1).reshape(2 * MODES, WIDTH)


def times_minus_i(value):
    low = low_lanes(value.shape[0])
    return jnp.concatenate([jnp.where(low, turn(tile), -turn(tile)) for tile in tiles(value)], axis=1)


def along_x(tables, value, sign):
    cos_high, cos_low, sin_high, sin_low = (table[...] for table in tables)
    straight = dot3(cos_high, cos_low, value)
    crossed = dot3(sin_high, sin_low, times_minus_i(value))
    return straight + crossed if sign < 0 else straight - crossed


def along_x_rounded(tables, value, sign):
    straight = dot(tables[0][...], value.astype(BF16))
    crossed = dot(tables[1][...], times_minus_i(value).astype(BF16))
    return straight + crossed if sign < 0 else straight - crossed


def first_kernel(volume, table_high, table_low, out):
    unit, _ = normalise(volume[...].astype(F32))
    to_owners(dot3(table_high[...], table_low[...], unit), out)


def filter_kernel(received, cos_high, cos_low, sin_high, sin_low, gain, w_in, b_in, w_out, b_out, sent, spectrum, inner, outer):
    tables = (cos_high, cos_low, sin_high, sin_low)
    unit_spectrum = along_x(tables, received[...], -1)
    spectrum[...] = unit_spectrum
    shrunk = []
    for block, part in enumerate(tiles(unit_spectrum * gain[...])):
        before = dot6(part, w_in[block]) + b_in[block]
        inner[block] = before
        after = dot6(gelu(before), w_out[block]) + b_out[block]
        outer[block] = after
        shrunk.append(after - jnp.clip(after, -SHRINK, SHRINK))
    sent[...] = along_x_rounded((cos_high, sin_high), jnp.concatenate(shrunk, axis=1), 1)


def packed_weight(grad):
    other = turn(grad[BLOCK:])
    return grad[:BLOCK] + jnp.where(low_lanes(BLOCK), other, -other)


SMALL = 32


def filter_back_kernel(received, cos, sin, gain, w_in, w_out, spectrum, inner, outer, sums, up_sum, sent, weights, small):
    tables = (cos, sin)
    unit_spectrum = spectrum[...]
    small[...] = jnp.zeros_like(small)
    grads = []
    scaled = tiles(unit_spectrum * gain[...])
    for block, grad_out in enumerate(tiles(along_x_rounded(tables, received[...], -1))):
        grad_out = jnp.where(jnp.abs(outer[block]) > SHRINK, grad_out, 0.0)
        active, slope = gelu_parts(inner[block])
        small[HALF + block : HALF + block + 1, :] = jnp.sum(grad_out, axis=0, keepdims=True)
        grad_out = grad_out.astype(BF16)
        weights[HALF + block] = packed_weight(dot_tn(active.astype(BF16), grad_out))
        grad_in = dot_nt(grad_out, w_out[block].astype(BF16)) * slope
        small[block : block + 1, :] = jnp.sum(grad_in, axis=0, keepdims=True)
        grad_in = grad_in.astype(BF16)
        weights[block] = packed_weight(dot_tn(scaled[block].astype(BF16), grad_in))
        grads.append(dot_nt(grad_in, w_in[block].astype(BF16)))
    grad = jnp.concatenate(grads, axis=1)
    for block, part in enumerate(tiles(jnp.sum(grad * unit_spectrum, axis=0, keepdims=True))):
        row = jnp.broadcast_to(part, (8, PAIR))
        small[6 + block : 7 + block, :] = (row + turn(row))[0:1, :]
    for at in range(3):
        lanes = slice(at * PAIR, (at + 1) * PAIR)
        small[9 + at : 10 + at, :] = sums[1:2, lanes]
        small[12 + at : 13 + at, :] = sums[0:1, lanes]
        small[15 + at : 16 + at, :] = sums[2:3, lanes]
    for at in range(HIDDEN // PAIR):
        small[18 + at : 19 + at, :] = up_sum[0:1, at * PAIR : (at + 1) * PAIR]
    sent[:, :, :WIDTH] = along_x_rounded(tables, grad, 1).reshape(GX, 8, WIDTH)
    for owner in range(GX):
        at = owner * 8
        sent[owner, :, WIDTH : WIDTH + PAIR] = weights[at // BLOCK, at % BLOCK : at % BLOCK + 8, :]
        at = GX * 8 + owner * 4
        sent[owner, 0:4, WIDTH + PAIR :] = weights[at // BLOCK, at % BLOCK : at % BLOCK + 4, :]
        if owner * 4 < SMALL:
            sent[owner, 4:8, WIDTH + PAIR :] = small[owner * 4 : owner * 4 + 4, :]
        else:
            sent[owner, 4:8, WIDTH + PAIR :] = jnp.zeros((4, PAIR), F32)


def mlp_kernel(volume, cotangent, modes, table, table_turned, gain_one, gain_two, up, up_bias, down,
               mixed, inputs, hidden, grad_before, grad_mixed, sent, up_sum, sums):
    weighted = (from_owners(modes[...]) * mode_weight()).astype(BF16)
    wide = volume[...].astype(F32)
    unit_one, _ = normalise(wide)
    mixed_here = wide + dot(table_turned[...], weighted) + unit_one * gain_one[...]
    mixed[...] = mixed_here
    unit_two, rate_two = normalise(mixed_here)
    inputs_here = (unit_two * gain_two[...]).astype(BF16)
    inputs[...] = inputs_here
    upstream = cotangent[...]
    up_sum[...] = jnp.zeros_like(up_sum)
    for at in range(0, HIDDEN, HBLOCK):
        cut = slice(at, at + HBLOCK)
        before = dot(inputs_here, up[:, cut]) + up_bias[:, cut]
        active, slope = gelu_parts(before)
        hidden[:, cut] = active.astype(BF16)
        back = (dot_nt(upstream, down[cut, :]) * slope).astype(BF16)
        grad_before[:, cut] = back
        up_sum[0:1, cut] = jnp.sum(back.astype(F32), axis=0, keepdims=True)
    grad = dot_nt(grad_before[...], up[...])
    upstream = upstream.astype(F32)
    grad_here = upstream + norm_back(grad * gain_two[...], unit_two, rate_two)
    grad_mixed[...] = grad_here
    sums[...] = jnp.zeros_like(sums)
    sums[0:1, :] = jnp.sum(grad * unit_two, axis=0, keepdims=True)
    sums[1:2, :] = jnp.sum(grad_here * unit_one, axis=0, keepdims=True)
    sums[2:3, :] = jnp.sum(upstream, axis=0, keepdims=True)
    to_owners(dot(table[...], grad_here.astype(BF16)) * mode_weight(), sent)


WBLOCK = 768


def weight_kernel(inputs, cotangent, hidden, grad_before, terms):
    for which, (left, right) in enumerate(((grad_before, inputs), (hidden, cotangent))):
        term = dot_tn(left[...], right[...])
        for place in range(WBLOCK // 96):
            for core in range(2):
                for half in range(2):
                    at = place * 96 + core * 48 + half * 24
                    terms[which * 2 + half, core, place] = term[at : at + 24, :]


def result_kernel(mixed, hidden, down, down_bias, result):
    result[...] = (mixed[...] + down_bias[...] + dot(hidden[...], down[...])).astype(BF16)


def last_kernel(volume, received, table_turned, gain_one, grad_mixed, out, rounded):
    @pl.when(pl.program_id(0) == 0)
    def _():
        rounded[...] = from_owners(received[:, :, :, :WIDTH]).astype(BF16)

    unit, rate = normalise(volume[...].astype(F32))
    here = grad_mixed[...]
    grad = dot(table_turned[...], rounded[...]) + here
    out[...] = (here + norm_back(grad * gain_one[...], unit, rate)).astype(BF16)


def first_sum_kernel(received, out):
    total = jnp.concatenate([jnp.sum(received[:, core, :, WIDTH:], axis=0) for core in range(2)], axis=1)
    for copy in range(8):
        out[copy] = total


def second_sum_kernel(received, terms, out):
    total = jnp.sum(received[...], axis=0)
    for place in range(PLACES):
        for group in range(3):
            out[place, :, group * WIDTH : (group + 1) * WIDTH] = terms[place, group * 8 : group * 8 + 8, :]
        out[place, :, 3 * WIDTH :] = total


def third_sum_kernel(received, out, slices):
    for group in range(3):
        total = jnp.sum(received[:, :, group * WIDTH : (group + 1) * WIDTH], axis=0)
        for copy in range(8):
            out[copy, group * 8 : group * 8 + 8, :] = total
    slices[...] = received[:, :, 3 * WIDTH :]


def weight_sum_kernel(received, grad_up, grad_down):
    parts = [received[2 * y] + received[2 * y + 1] for y in range(4)]
    grad_up[...] = jnp.concatenate(parts[:2], axis=0)
    grad_down[...] = jnp.concatenate(parts[2:], axis=0)


def final_kernel(core, mine, other, grad_w_in, grad_w_out, grad_b_in, grad_b_out, grad_one, grad_two, grad_down_bias, grad_up_bias, weights, small):
    first = core[0] == 0
    both = (jnp.where(first, mine[...], other[...]), jnp.where(first, other[...], mine[...]))
    for owner in range(GX):
        piece = both[owner % 2][owner // 2]
        for half in range(2):
            lanes = 2 * PAIR * half
            weights[half, owner * 8 : owner * 8 + 8, :] = piece[:, lanes : lanes + PAIR]
            at = GX * 8 + owner * 4
            weights[half, at : at + 4, :] = piece[0:4, lanes + PAIR : lanes + 2 * PAIR]
            if owner * 4 < SMALL:
                small[half, owner * 4 : owner * 4 + 4, :] = piece[4:8, lanes + PAIR : lanes + 2 * PAIR]
    for which, out in enumerate((grad_w_in, grad_w_out)):
        for block in range(BLOCKS):
            at = (which * HALF + block % HALF) * BLOCK
            part = weights[block // HALF, at : at + BLOCK, :]
            out[0, block] = part[:, :BLOCK]
            out[1, block] = part[:, BLOCK:]
    for first_row, out in ((0, grad_b_in), (HALF, grad_b_out)):
        for block in range(BLOCKS):
            row = small[block // HALF, first_row + block % HALF : first_row + block % HALF + 1, :]
            out[block, 0:1, :] = row[:, :BLOCK]
            out[block, 1:2, :] = row[:, BLOCK:]
    tokens = small[0] + small[1]
    low = low_lanes(1)
    for at in range(3):
        even, odd = (small[block // HALF, 6 + block % HALF : 7 + block % HALF, :] for block in (2 * at, 2 * at + 1))
        row = tokens[9 + at : 10 + at, :] + jnp.where(low, even, odd)
        grad_one[at * PAIR : (at + 1) * PAIR] = row[0]
    for first_row, out in ((12, grad_two), (15, grad_down_bias), (18, grad_up_bias)):
        for at in range(out.shape[0] // PAIR):
            out[at * PAIR : (at + 1) * PAIR] = tokens[first_row + at]


def limit(mib):
    return pltpu.CompilerParams(vmem_limit_bytes=mib * MIB)


def call(kernel, out, *operands, mib=12):
    return pl.pallas_call(kernel, out_shape=out, compiler_params=limit(mib))(*operands)


def exchange(value, axis, groups=None):
    return lax.all_to_all(value, axis, split_axis=0, concat_axis=0, axis_index_groups=groups, tiled=True)


def paired(weight, core):
    weight = lax.dynamic_slice_in_dim(weight, core * HALF, HALF, 1)
    top = jnp.concatenate([weight[0], weight[1]], axis=2)
    return jnp.concatenate([top, jnp.concatenate([-weight[1], weight[0]], axis=2)], axis=1)


def paired_bias(bias, core):
    bias = lax.dynamic_slice_in_dim(bias, core * HALF, HALF, 1)
    return bias.transpose(1, 0, 2).reshape(HALF, 1, PAIR)


def local(volume, gain_one, gain_two, w_in, b_in, w_out, b_out, up, up_bias, down, down_bias, cotangent):
    shape = volume.shape
    volume = volume.reshape(TOKENS, WIDTH)
    cotangent = cotangent.reshape(TOKENS, WIDTH)
    gain_one, gain_two, down_bias = (value.reshape(1, WIDTH) for value in (gain_one, gain_two, down_bias))
    slab = slab_table()
    slab_high, slab_low = (jnp.asarray(part) for part in halves(slab))
    slab_turned = jnp.asarray(halves(slab.T)[0])
    cross = [jnp.asarray(part) for table in cross_tables() for part in halves(table)]
    core = lax.axis_index("space") & 1
    w_in, w_out, b_in, b_out = paired(w_in, core), paired(w_out, core), paired_bias(b_in, core), paired_bias(b_out, core)
    gain = lax.dynamic_slice_in_dim(gain_one.reshape(BLOCKS, 1, BLOCK), core * HALF, HALF, 0)
    gain = jnp.broadcast_to(gain, (HALF, 2, BLOCK)).reshape(1, WIDTH)

    def sds(*dims, dtype=F32):
        return jax.ShapeDtypeStruct(dims, dtype)

    def rows(value):
        return value.reshape(2 * MODES, WIDTH)

    def places(value):
        return value.reshape(PLACES, 2, OWN, value.shape[-1])

    def owners(value):
        return value.reshape(GX, OWN, WIDTH)

    wave = sds(PLACES, 2, OWN, WIDTH)
    modes = call(first_kernel, wave, volume, slab_high, slab_low, mib=60)
    modes = rows(exchange(owners(modes), "space"))
    wide = sds(HALF, 2 * MODES, PAIR)
    modes, spectrum, inner, outer = call(
        filter_kernel, (sds(2 * MODES, WIDTH), sds(2 * MODES, WIDTH), wide, wide), modes, *cross, gain, w_in, b_in, w_out, b_out
    )
    modes = places(exchange(owners(modes), "space"))

    def whole(*dims):
        return pl.BlockSpec(dims, lambda step: (0,) * len(dims))

    def chunk(*dims):
        return pl.BlockSpec(dims, lambda step: (step, 0))

    def across(*dims):
        return pl.BlockSpec(dims, lambda step: (0, step))

    mixed, inputs, hidden, grad_before, grad_mixed, modes, up_sum, sums = call(
        mlp_kernel,
        (
            sds(TOKENS, WIDTH), sds(TOKENS, WIDTH, dtype=BF16), sds(TOKENS, HIDDEN, dtype=BF16), sds(TOKENS, HIDDEN, dtype=BF16),
            sds(TOKENS, WIDTH), wave, sds(8, HIDDEN), sds(8, WIDTH),
        ),
        volume, cotangent, modes, slab_high, slab_turned, gain_one, gain_two, up, up_bias.reshape(1, HIDDEN), down,
        mib=60,
    )

    terms = pl.pallas_call(
        weight_kernel,
        grid=(HIDDEN // WBLOCK,),
        in_specs=[whole(TOKENS, WIDTH), whole(TOKENS, WIDTH), across(TOKENS, WBLOCK), across(TOKENS, WBLOCK)],
        out_specs=pl.BlockSpec((4, 2, WBLOCK // 96, 24, WIDTH), lambda step: (0, 0, step, 0, 0)),
        out_shape=sds(4, 2, PLACES, 24, WIDTH),
        compiler_params=limit(60),
        cost_estimate=pl.CostEstimate(flops=4 * TOKENS * WIDTH * HIDDEN, bytes_accessed=12 * MIB, transcendentals=0),
    )(inputs, cotangent, hidden, grad_before)
    result = pl.pallas_call(
        result_kernel,
        grid=(TOKENS // CHUNK,),
        in_specs=[chunk(CHUNK, WIDTH), chunk(CHUNK, HIDDEN), whole(HIDDEN, WIDTH), whole(1, WIDTH)],
        out_specs=chunk(CHUNK, WIDTH),
        out_shape=sds(TOKENS, WIDTH, dtype=BF16),
        compiler_params=limit(60),
        cost_estimate=pl.CostEstimate(flops=2 * TOKENS * WIDTH * HIDDEN, bytes_accessed=7 * MIB, transcendentals=0),
    )(mixed, hidden, down, down_bias)

    modes = exchange(owners(modes), "space")
    terms = lax.psum_scatter(
        terms.reshape(8, PLACES * 24, WIDTH), ("dp", "space"), scatter_dimension=0, axis_index_groups=Y_CORE, tiled=True
    ).reshape(PLACES, 24, WIDTH)
    modes = rows(modes)
    carried = 2 * PAIR
    sent = pl.pallas_call(
        filter_back_kernel,
        out_shape=sds(GX, 8, WIDTH + carried),
        scratch_shapes=[pltpu.VMEM((2 * HALF, BLOCK, PAIR), F32), pltpu.VMEM((SMALL, PAIR), F32)],
        compiler_params=limit(12),
        cost_estimate=pl.CostEstimate(flops=LATE, bytes_accessed=8 * MIB, transcendentals=0),
    )(modes, cross[0], cross[2], gain, w_in, w_out, spectrum, inner, outer, sums, up_sum)
    received = places(exchange(sent, "space"))
    shared = exchange(call(first_sum_kernel, sds(8, 8, 2 * carried), received), "dp")
    grad_volume = pl.pallas_call(
        last_kernel,
        grid=(TOKENS // CHUNK,),
        in_specs=[
            chunk(CHUNK, WIDTH), whole(PLACES, 2, OWN, WIDTH + carried), chunk(CHUNK, 2 * MODES), whole(1, WIDTH), chunk(CHUNK, WIDTH),
        ],
        out_specs=chunk(CHUNK, WIDTH),
        out_shape=sds(TOKENS, WIDTH, dtype=BF16),
        scratch_shapes=[pltpu.VMEM((2 * MODES, WIDTH), BF16)],
        compiler_params=limit(12),
        cost_estimate=pl.CostEstimate(flops=TOKENS * WIDTH * 1024, bytes_accessed=8 * 1024 * 1024, transcendentals=0),
    )(volume, received, slab_turned, gain_one, grad_mixed)
    shared, result, grad_volume = lax.optimization_barrier((shared, result, grad_volume))
    gathered = exchange(call(second_sum_kernel, sds(PLACES, 8, 3 * WIDTH + 2 * carried), shared, terms), "space", X_Z)
    copies, mine = call(third_sum_kernel, (sds(8, 24, WIDTH), sds(PLACES, 8, 2 * carried)), gathered)
    other = lax.ppermute(mine, "space", [(at, at ^ 1) for at in range(GX)])
    copies = exchange(copies, "dp")
    square = sds(2, BLOCKS, BLOCK, BLOCK)
    vmem = pl.BlockSpec(memory_space=pltpu.VMEM)
    tall = sds(BLOCKS, 2, BLOCK)
    row = sds(WIDTH)
    grad_up, grad_down = call(weight_sum_kernel, (sds(48, WIDTH), sds(48, WIDTH)), copies)
    grad_w_in, grad_w_out, grad_b_in, grad_b_out, grad_one, grad_two, grad_down_bias, grad_up_bias = pl.pallas_call(
        final_kernel,
        in_specs=[pl.BlockSpec(memory_space=pltpu.SMEM), vmem, vmem],
        out_shape=(square, square, tall, tall, row, row, row, sds(HIDDEN)),
        scratch_shapes=[pltpu.VMEM((2, 2 * HALF * BLOCK, PAIR), F32), pltpu.VMEM((2, SMALL, PAIR), F32)],
        compiler_params=limit(60),
    )(core.reshape(1), mine, other)
    return (
        result.reshape(shape),
        grad_volume.reshape(shape),
        grad_one,
        grad_two,
        grad_w_in,
        grad_b_in.transpose(1, 0, 2),
        grad_w_out,
        grad_b_out.transpose(1, 0, 2),
        grad_up.T,
        grad_up_bias,
        grad_down,
        grad_down_bias,
    )


def solution(mesh):
    field = P("dp", "space", None, None, None)
    return jax.shard_map(
        local,
        mesh=mesh,
        in_specs=(field,) + (P(),) * 10 + (field,),
        out_specs=(field, field) + (P(),) * 6 + (P(None, "space"), P(), P("space", None), P()),
        check_vma=False,
    )
```

```python
import functools
import math

import jax
import jax.numpy as jnp
import ml_dtypes
import numpy as np
from jax import lax
from jax.experimental import pallas as pl
from jax.experimental.pallas import tpu as pltpu
from jax.sharding import PartitionSpec as P

WIDTH = 384
BLOCKS = 6
BLOCK = 64
HIDDEN = 1536
GX = 32
GY = 32
GZ = 32
KEEP_Y = 16
KEEP_Z = 8
MODES = KEEP_Y * KEEP_Z
PLACES = GX // 2
OWN = MODES // PLACES
TOKENS = GY * GZ
HALF = BLOCKS // 2
PAIR = 2 * BLOCK
HBLOCK = 768
CHUNK = 512

Y_CORE = [
    [(y * 2 + low) * GX + place * 2 + core for y in range(4) for core in range(2)] for low in range(2) for place in range(GX // 2)
]
X_Z = [[place * 2 + core for place in range(GX // 2)] for core in range(2)]

EPSILON = 1e-05
SHRINK = 0.01
ROOT = math.sqrt(2.0 / math.pi)
CUBIC = 0.044715 * ROOT
MIB = 1024 * 1024
LATE = 200_000_000_000

BF16 = jnp.bfloat16
F32 = jnp.float32


def halves(table):
    high = table.astype(np.float32).astype(ml_dtypes.bfloat16)
    low = (table - high.astype(np.float64)).astype(np.float32).astype(ml_dtypes.bfloat16)
    return high, low


def slab_table():
    kept = np.concatenate([np.arange(KEEP_Y // 2), np.arange(GY - KEEP_Y // 2, GY)])
    ky, kz = np.repeat(kept, KEEP_Z), np.tile(np.arange(KEEP_Z), KEEP_Y)
    y, z = np.repeat(np.arange(GY), GZ), np.tile(np.arange(GZ), GY)
    angle = 2.0 * np.pi * ((ky[:, None] * y[None, :] + kz[:, None] * z[None, :]) % GY) / GY
    both = np.stack([np.cos(angle), -np.sin(angle)]).reshape(2, PLACES, OWN, TOKENS)
    return both.transpose(1, 0, 2, 3).reshape(2 * MODES, TOKENS) / math.sqrt(TOKENS)


def cross_tables():
    angle = 2.0 * np.pi * (np.outer(np.arange(GX), np.arange(GX)) % GX) / GX
    return [np.kron(part(angle), np.eye(OWN)) / math.sqrt(GX) for part in (np.cos, np.sin)]


def dot(a, b):
    return jnp.dot(a, b, preferred_element_type=F32)


def dot_nt(a, b):
    return lax.dot_general(a, b, (((1,), (1,)), ((), ())), preferred_element_type=F32)


def dot_tn(a, b):
    return lax.dot_general(a, b, (((0,), (0,)), ((), ())), preferred_element_type=F32)


def split(value):
    high = value.astype(BF16)
    return high, (value - high.astype(F32)).astype(BF16)


def dot3(table, value):
    high, low = split(value)
    rows = table.shape[0] // 2
    both = dot(table, high)
    return both[:rows] + (both[rows:] + dot(table[:rows], low))


def dot6(a, b):
    return jnp.dot(a, b, preferred_element_type=F32, precision=lax.Precision.HIGHEST)


def normalise(values):
    center = values - jnp.mean(values, axis=-1, keepdims=True)
    rate = lax.rsqrt(jnp.mean(center * center, axis=-1, keepdims=True) + EPSILON)
    return center * rate, rate


def norm_back(grad, unit, rate):
    first = jnp.mean(grad, axis=-1, keepdims=True)
    second = jnp.mean(grad * unit, axis=-1, keepdims=True)
    return rate * (grad - first - unit * second)


def gelu_parts(value):
    square = value * value
    gate = 0.5 + 0.5 * jnp.tanh(value * (ROOT + CUBIC * square))
    active = value * gate
    slope = gate + (active - active * gate) * (2.0 * ROOT + (6.0 * CUBIC) * square)
    return active, slope


def gelu(value):
    return value * (0.5 + 0.5 * jnp.tanh(value * (ROOT + CUBIC * (value * value))))


def mode_weight():
    place = lax.broadcasted_iota(jnp.int32, (2 * MODES, 1), 0) & (KEEP_Z - 1)
    return jnp.where(place == 0, 1.0, 2.0).astype(F32)


def low_lanes(rows):
    return lax.broadcasted_iota(jnp.int32, (rows, PAIR), 1) < BLOCK


def turn(tile):
    return pltpu.roll(tile, BLOCK, 1)


def tiles(value):
    return [value[:, at : at + PAIR] for at in range(0, value.shape[1], PAIR)]


def to_owners(value, out):
    value = value.reshape(PLACES, 2, OWN, WIDTH)
    low = low_lanes(MODES)
    for at, (real, imag) in enumerate(zip(tiles(value[:, 0].reshape(MODES, WIDTH)), tiles(value[:, 1].reshape(MODES, WIDTH)))):
        for block, tile in ((2 * at, jnp.where(low, real, turn(imag))), (2 * at + 1, jnp.where(low, turn(real), imag))):
            lanes = (block % HALF) * PAIR
            out[:, block // HALF, :, lanes : lanes + PAIR] = tile.reshape(PLACES, OWN, PAIR)


def from_owners(value):
    low = low_lanes(MODES)
    blocks = [tile for core in range(2) for tile in tiles(value[:, core].reshape(MODES, WIDTH))]
    real = [jnp.where(low, even, turn(odd)) for even, odd in zip(blocks[0::2], blocks[1::2])]
    imag = [jnp.where(low, turn(even), odd) for even, odd in zip(blocks[0::2], blocks[1::2])]
    parts = [jnp.concatenate(part, axis=1).reshape(PLACES, 1, OWN, WIDTH) for part in (real, imag)]
    return jnp.concatenate(parts, axis=1).reshape(2 * MODES, WIDTH)


def times_minus_i(value):
    low = low_lanes(value.shape[0])
    return jnp.concatenate([jnp.where(low, turn(tile), -turn(tile)) for tile in tiles(value)], axis=1)


def along_x(tables, value, sign):
    straight = dot3(tables[0][...], value)
    crossed = dot3(tables[1][...], times_minus_i(value))
    return straight + crossed if sign < 0 else straight - crossed


def along_x_rounded(tables, value, sign):
    straight = dot(tables[0][...], value.astype(BF16))
    crossed = dot(tables[1][...], times_minus_i(value).astype(BF16))
    return straight + crossed if sign < 0 else straight - crossed


def first_kernel(volume, table, out):
    unit, _ = normalise(volume[...].astype(F32))
    to_owners(dot3(table[...], unit), out)


def filter_kernel(received, cos, sin, gain, w_in, b_in, w_out, b_out, sent, spectrum, inner, outer):
    tables = (cos, sin)
    unit_spectrum = along_x(tables, received[...], -1)
    spectrum[...] = unit_spectrum
    shrunk = []
    for block, part in enumerate(tiles(unit_spectrum * gain[...])):
        before = dot6(part, w_in[block]) + b_in[block]
        inner[block] = before
        after = dot6(gelu(before), w_out[block]) + b_out[block]
        outer[block] = after
        shrunk.append(after - jnp.clip(after, -SHRINK, SHRINK))
    sent[...] = along_x_rounded([table[: 2 * MODES] for table in tables], jnp.concatenate(shrunk, axis=1), 1)


def packed_weight(grad):
    other = turn(grad[BLOCK:])
    return grad[:BLOCK] + jnp.where(low_lanes(BLOCK), other, -other)


SMALL = 32


def filter_back_kernel(received, cos, sin, gain, w_in, w_out, spectrum, inner, outer, sums, up_sum, sent, weights, small):
    tables = (cos, sin)
    unit_spectrum = spectrum[...]
    small[...] = jnp.zeros_like(small)
    grads = []
    scaled = tiles(unit_spectrum * gain[...])
    for block, grad_out in enumerate(tiles(along_x_rounded(tables, received[...], -1))):
        grad_out = jnp.where(jnp.abs(outer[block]) > SHRINK, grad_out, 0.0)
        active, slope = gelu_parts(inner[block])
        small[HALF + block : HALF + block + 1, :] = jnp.sum(grad_out, axis=0, keepdims=True)
        grad_out = grad_out.astype(BF16)
        weights[HALF + block] = packed_weight(dot_tn(active.astype(BF16), grad_out))
        grad_in = dot_nt(grad_out, w_out[block].astype(BF16)) * slope
        small[block : block + 1, :] = jnp.sum(grad_in, axis=0, keepdims=True)
        grad_in = grad_in.astype(BF16)
        weights[block] = packed_weight(dot_tn(scaled[block].astype(BF16), grad_in))
        grads.append(dot_nt(grad_in, w_in[block].astype(BF16)))
    grad = jnp.concatenate(grads, axis=1)
    for block, part in enumerate(tiles(jnp.sum(grad * unit_spectrum, axis=0, keepdims=True))):
        row = jnp.broadcast_to(part, (8, PAIR))
        small[6 + block : 7 + block, :] = (row + turn(row))[0:1, :]
    for at in range(3):
        lanes = slice(at * PAIR, (at + 1) * PAIR)
        small[9 + at : 10 + at, :] = sums[1:2, lanes]
        small[12 + at : 13 + at, :] = sums[0:1, lanes]
        small[15 + at : 16 + at, :] = sums[2:3, lanes]
    for at in range(HIDDEN // PAIR):
        small[18 + at : 19 + at, :] = up_sum[0:1, at * PAIR : (at + 1) * PAIR]
    sent[:, :, :WIDTH] = along_x_rounded(tables, grad, 1).reshape(GX, 8, WIDTH)
    for owner in range(GX):
        at = owner * 8
        sent[owner, :, WIDTH : WIDTH + PAIR] = weights[at // BLOCK, at % BLOCK : at % BLOCK + 8, :]
        at = GX * 8 + owner * 4
        sent[owner, 0:4, WIDTH + PAIR :] = weights[at // BLOCK, at % BLOCK : at % BLOCK + 4, :]
        if owner * 4 < SMALL:
            sent[owner, 4:8, WIDTH + PAIR :] = small[owner * 4 : owner * 4 + 4, :]
        else:
            sent[owner, 4:8, WIDTH + PAIR :] = jnp.zeros((4, PAIR), F32)


def mlp_kernel(volume, cotangent, modes, table, table_turned, gain_one, gain_two, up, up_bias, down,
               mixed, inputs, hidden, grad_before, grad_mixed, sent, up_sum, sums):
    weighted = (from_owners(modes[...]) * mode_weight()).astype(BF16)
    wide = volume[...].astype(F32)
    unit_one, _ = normalise(wide)
    mixed_here = wide + dot(table_turned[...], weighted) + unit_one * gain_one[...]
    mixed[...] = mixed_here
    unit_two, rate_two = normalise(mixed_here)
    inputs_here = (unit_two * gain_two[...]).astype(BF16)
    inputs[...] = inputs_here
    upstream = cotangent[...]
    up_sum[...] = jnp.zeros_like(up_sum)
    for at in range(0, HIDDEN, HBLOCK):
        cut = slice(at, at + HBLOCK)
        before = dot(inputs_here, up[:, cut]) + up_bias[:, cut]
        active, slope = gelu_parts(before)
        hidden[:, cut] = active.astype(BF16)
        back = (dot_nt(upstream, down[cut, :]) * slope).astype(BF16)
        grad_before[:, cut] = back
        up_sum[0:1, cut] = jnp.sum(back.astype(F32), axis=0, keepdims=True)
    grad = dot_nt(grad_before[...], up[...])
    upstream = upstream.astype(F32)
    grad_here = upstream + norm_back(grad * gain_two[...], unit_two, rate_two)
    grad_mixed[...] = grad_here
    sums[...] = jnp.zeros_like(sums)
    sums[0:1, :] = jnp.sum(grad * unit_two, axis=0, keepdims=True)
    sums[1:2, :] = jnp.sum(grad_here * unit_one, axis=0, keepdims=True)
    sums[2:3, :] = jnp.sum(upstream, axis=0, keepdims=True)
    to_owners(dot(table[...], grad_here.astype(BF16)) * mode_weight(), sent)


WBLOCK = 768


def weight_kernel(inputs, cotangent, hidden, grad_before, terms):
    for which, (left, right) in enumerate(((grad_before, inputs), (hidden, cotangent))):
        term = dot_tn(left[...], right[...])
        for place in range(WBLOCK // 96):
            for core in range(2):
                for half in range(2):
                    at = place * 96 + core * 48 + half * 24
                    terms[which * 2 + half, core, place] = term[at : at + 24, :]


def result_kernel(mixed, hidden, down, down_bias, result):
    result[...] = (mixed[...] + down_bias[...] + dot(hidden[...], down[...])).astype(BF16)


def last_kernel(volume, received, table_turned, gain_one, grad_mixed, out, rounded):
    @pl.when(pl.program_id(0) == 0)
    def _():
        rounded[...] = from_owners(received[:, :, :, :WIDTH]).astype(BF16)

    unit, rate = normalise(volume[...].astype(F32))
    here = grad_mixed[...]
    grad = dot(table_turned[...], rounded[...]) + here
    out[...] = (here + norm_back(grad * gain_one[...], unit, rate)).astype(BF16)


def first_sum_kernel(received, out):
    total = jnp.concatenate([jnp.sum(received[:, core, :, WIDTH:], axis=0) for core in range(2)], axis=1)
    for copy in range(8):
        out[copy] = total


def second_sum_kernel(received, terms, out):
    total = jnp.sum(received[...], axis=0)
    for place in range(PLACES):
        for group in range(3):
            out[place, :, group * WIDTH : (group + 1) * WIDTH] = terms[place, group * 8 : group * 8 + 8, :]
        out[place, :, 3 * WIDTH :] = total


def third_sum_kernel(received, out, slices):
    for group in range(3):
        total = jnp.sum(received[:, :, group * WIDTH : (group + 1) * WIDTH], axis=0)
        for copy in range(8):
            out[copy, group * 8 : group * 8 + 8, :] = total
    slices[...] = received[:, :, 3 * WIDTH :]


def weight_sum_kernel(received, grad_up, grad_down):
    parts = [received[2 * y] + received[2 * y + 1] for y in range(4)]
    grad_up[...] = jnp.concatenate(parts[:2], axis=0)
    grad_down[...] = jnp.concatenate(parts[2:], axis=0)


def final_kernel(core, mine, other, grad_w_in, grad_w_out, grad_b_in, grad_b_out, grad_one, grad_two, grad_down_bias, grad_up_bias, weights, small):
    first = core[0] == 0
    both = (jnp.where(first, mine[...], other[...]), jnp.where(first, other[...], mine[...]))
    for owner in range(GX):
        piece = both[owner % 2][owner // 2]
        for half in range(2):
            lanes = 2 * PAIR * half
            weights[half, owner * 8 : owner * 8 + 8, :] = piece[:, lanes : lanes + PAIR]
            at = GX * 8 + owner * 4
            weights[half, at : at + 4, :] = piece[0:4, lanes + PAIR : lanes + 2 * PAIR]
            if owner * 4 < SMALL:
                small[half, owner * 4 : owner * 4 + 4, :] = piece[4:8, lanes + PAIR : lanes + 2 * PAIR]
    for which, out in enumerate((grad_w_in, grad_w_out)):
        for block in range(BLOCKS):
            at = (which * HALF + block % HALF) * BLOCK
            part = weights[block // HALF, at : at + BLOCK, :]
            out[0, block] = part[:, :BLOCK]
            out[1, block] = part[:, BLOCK:]
    for first_row, out in ((0, grad_b_in), (HALF, grad_b_out)):
        for block in range(BLOCKS):
            row = small[block // HALF, first_row + block % HALF : first_row + block % HALF + 1, :]
            out[block, 0:1, :] = row[:, :BLOCK]
            out[block, 1:2, :] = row[:, BLOCK:]
    tokens = small[0] + small[1]
    low = low_lanes(1)
    for at in range(3):
        even, odd = (small[block // HALF, 6 + block % HALF : 7 + block % HALF, :] for block in (2 * at, 2 * at + 1))
        row = tokens[9 + at : 10 + at, :] + jnp.where(low, even, odd)
        grad_one[at * PAIR : (at + 1) * PAIR] = row[0]
    for first_row, out in ((12, grad_two), (15, grad_down_bias), (18, grad_up_bias)):
        for at in range(out.shape[0] // PAIR):
            out[at * PAIR : (at + 1) * PAIR] = tokens[first_row + at]


def limit(mib):
    return pltpu.CompilerParams(vmem_limit_bytes=mib * MIB)


def call(kernel, out, *operands, mib=12):
    return pl.pallas_call(kernel, out_shape=out, compiler_params=limit(mib))(*operands)


def exchange(value, axis, groups=None):
    return lax.all_to_all(value, axis, split_axis=0, concat_axis=0, axis_index_groups=groups, tiled=True)


def paired(weight, core):
    weight = lax.dynamic_slice_in_dim(weight, core * HALF, HALF, 1)
    top = jnp.concatenate([weight[0], weight[1]], axis=2)
    return jnp.concatenate([top, jnp.concatenate([-weight[1], weight[0]], axis=2)], axis=1)


def paired_bias(bias, core):
    bias = lax.dynamic_slice_in_dim(bias, core * HALF, HALF, 1)
    return bias.transpose(1, 0, 2).reshape(HALF, 1, PAIR)


def local(volume, gain_one, gain_two, w_in, b_in, w_out, b_out, up, up_bias, down, down_bias, cotangent):
    shape = volume.shape
    volume = volume.reshape(TOKENS, WIDTH)
    cotangent = cotangent.reshape(TOKENS, WIDTH)
    gain_one, gain_two, down_bias = (value.reshape(1, WIDTH) for value in (gain_one, gain_two, down_bias))
    slab = slab_table()
    slab_high, slab_both = jnp.asarray(halves(slab)[0]), jnp.asarray(np.concatenate(halves(slab)))
    slab_turned = jnp.asarray(halves(slab.T)[0])
    cross = [jnp.asarray(np.concatenate(halves(table))) for table in cross_tables()]
    cross_high = [jnp.asarray(halves(table)[0]) for table in cross_tables()]
    core = lax.axis_index("space") & 1
    w_in, w_out, b_in, b_out = paired(w_in, core), paired(w_out, core), paired_bias(b_in, core), paired_bias(b_out, core)
    gain = lax.dynamic_slice_in_dim(gain_one.reshape(BLOCKS, 1, BLOCK), core * HALF, HALF, 0)
    gain = jnp.broadcast_to(gain, (HALF, 2, BLOCK)).reshape(1, WIDTH)

    def sds(*dims, dtype=F32):
        return jax.ShapeDtypeStruct(dims, dtype)

    def rows(value):
        return value.reshape(2 * MODES, WIDTH)

    def places(value):
        return value.reshape(PLACES, 2, OWN, value.shape[-1])

    def owners(value):
        return value.reshape(GX, OWN, WIDTH)

    wave = sds(PLACES, 2, OWN, WIDTH)
    modes = call(first_kernel, wave, volume, slab_both, mib=60)
    modes = rows(exchange(owners(modes), "space"))
    wide = sds(HALF, 2 * MODES, PAIR)
    modes, spectrum, inner, outer = call(
        filter_kernel, (sds(2 * MODES, WIDTH), sds(2 * MODES, WIDTH), wide, wide), modes, *cross, gain, w_in, b_in, w_out, b_out
    )
    modes = places(exchange(owners(modes), "space"))

    def whole(*dims):
        return pl.BlockSpec(dims, lambda step: (0,) * len(dims))

    def chunk(*dims):
        return pl.BlockSpec(dims, lambda step: (step, 0))

    def across(*dims):
        return pl.BlockSpec(dims, lambda step: (0, step))

    mixed, inputs, hidden, grad_before, grad_mixed, modes, up_sum, sums = call(
        mlp_kernel,
        (
            sds(TOKENS, WIDTH), sds(TOKENS, WIDTH, dtype=BF16), sds(TOKENS, HIDDEN, dtype=BF16), sds(TOKENS, HIDDEN, dtype=BF16),
            sds(TOKENS, WIDTH), wave, sds(8, HIDDEN), sds(8, WIDTH),
        ),
        volume, cotangent, modes, slab_high, slab_turned, gain_one, gain_two, up, up_bias.reshape(1, HIDDEN), down,
        mib=60,
    )

    terms = pl.pallas_call(
        weight_kernel,
        grid=(HIDDEN // WBLOCK,),
        in_specs=[whole(TOKENS, WIDTH), whole(TOKENS, WIDTH), across(TOKENS, WBLOCK), across(TOKENS, WBLOCK)],
        out_specs=pl.BlockSpec((4, 2, WBLOCK // 96, 24, WIDTH), lambda step: (0, 0, step, 0, 0)),
        out_shape=sds(4, 2, PLACES, 24, WIDTH),
        compiler_params=limit(60),
        cost_estimate=pl.CostEstimate(flops=4 * TOKENS * WIDTH * HIDDEN, bytes_accessed=12 * MIB, transcendentals=0),
    )(inputs, cotangent, hidden, grad_before)
    result = pl.pallas_call(
        result_kernel,
        grid=(TOKENS // CHUNK,),
        in_specs=[chunk(CHUNK, WIDTH), chunk(CHUNK, HIDDEN), whole(HIDDEN, WIDTH), whole(1, WIDTH)],
        out_specs=chunk(CHUNK, WIDTH),
        out_shape=sds(TOKENS, WIDTH, dtype=BF16),
        compiler_params=limit(60),
        cost_estimate=pl.CostEstimate(flops=2 * TOKENS * WIDTH * HIDDEN, bytes_accessed=7 * MIB, transcendentals=0),
    )(mixed, hidden, down, down_bias)

    modes = exchange(owners(modes), "space")
    terms = lax.psum_scatter(
        terms.reshape(8, PLACES * 24, WIDTH), ("dp", "space"), scatter_dimension=0, axis_index_groups=Y_CORE, tiled=True
    ).reshape(PLACES, 24, WIDTH)
    modes = rows(modes)
    carried = 2 * PAIR
    sent = pl.pallas_call(
        filter_back_kernel,
        out_shape=sds(GX, 8, WIDTH + carried),
        scratch_shapes=[pltpu.VMEM((2 * HALF, BLOCK, PAIR), F32), pltpu.VMEM((SMALL, PAIR), F32)],
        compiler_params=limit(12),
        cost_estimate=pl.CostEstimate(flops=LATE, bytes_accessed=8 * MIB, transcendentals=0),
    )(modes, *cross_high, gain, w_in, w_out, spectrum, inner, outer, sums, up_sum)
    received = places(exchange(sent, "space"))
    shared = exchange(call(first_sum_kernel, sds(8, 8, 2 * carried), received), "dp")
    grad_volume = pl.pallas_call(
        last_kernel,
        grid=(TOKENS // CHUNK,),
        in_specs=[
            chunk(CHUNK, WIDTH), whole(PLACES, 2, OWN, WIDTH + carried), chunk(CHUNK, 2 * MODES), whole(1, WIDTH), chunk(CHUNK, WIDTH),
        ],
        out_specs=chunk(CHUNK, WIDTH),
        out_shape=sds(TOKENS, WIDTH, dtype=BF16),
        scratch_shapes=[pltpu.VMEM((2 * MODES, WIDTH), BF16)],
        compiler_params=limit(12),
        cost_estimate=pl.CostEstimate(flops=TOKENS * WIDTH * 1024, bytes_accessed=8 * 1024 * 1024, transcendentals=0),
    )(volume, received, slab_turned, gain_one, grad_mixed)
    shared, result, grad_volume = lax.optimization_barrier((shared, result, grad_volume))
    gathered = exchange(call(second_sum_kernel, sds(PLACES, 8, 3 * WIDTH + 2 * carried), shared, terms), "space", X_Z)
    copies, mine = call(third_sum_kernel, (sds(8, 24, WIDTH), sds(PLACES, 8, 2 * carried)), gathered)
    other = lax.ppermute(mine, "space", [(at, at ^ 1) for at in range(GX)])
    copies = exchange(copies, "dp")
    square = sds(2, BLOCKS, BLOCK, BLOCK)
    vmem = pl.BlockSpec(memory_space=pltpu.VMEM)
    tall = sds(BLOCKS, 2, BLOCK)
    row = sds(WIDTH)
    grad_up, grad_down = call(weight_sum_kernel, (sds(48, WIDTH), sds(48, WIDTH)), copies)
    grad_w_in, grad_w_out, grad_b_in, grad_b_out, grad_one, grad_two, grad_down_bias, grad_up_bias = pl.pallas_call(
        final_kernel,
        in_specs=[pl.BlockSpec(memory_space=pltpu.SMEM), vmem, vmem],
        out_shape=(square, square, tall, tall, row, row, row, sds(HIDDEN)),
        scratch_shapes=[pltpu.VMEM((2, 2 * HALF * BLOCK, PAIR), F32), pltpu.VMEM((2, SMALL, PAIR), F32)],
        compiler_params=limit(60),
    )(core.reshape(1), mine, other)
    return (
        result.reshape(shape),
        grad_volume.reshape(shape),
        grad_one,
        grad_two,
        grad_w_in,
        grad_b_in.transpose(1, 0, 2),
        grad_w_out,
        grad_b_out.transpose(1, 0, 2),
        grad_up.T,
        grad_up_bias,
        grad_down,
        grad_down_bias,
    )


def solution(mesh):
    field = P("dp", "space", None, None, None)
    return jax.shard_map(
        local,
        mesh=mesh,
        in_specs=(field,) + (P(),) * 10 + (field,),
        out_specs=(field, field) + (P(),) * 6 + (P(None, "space"), P(), P("space", None), P()),
        check_vma=False,
    )
```
